256 devices in a mesh: seq: 32 (over z, y_lo, core), head: 8 (over y_hi, x).
Axes of the slice: x: 4, y: 4 (y_hi: 2, y_lo: 2; y = y_hi * 2 + y_lo), z: 8, core: 2. Of those that a mesh axis runs over, the one named last changes fastest.
Arguments:
- comp_q: bfloat16 [32, 192, 8, 640], P('seq', 'head'), may hold values from -8 to 8
- comp_k: bfloat16 [32, 192, 8, 128], P('seq', 'head'), may hold values from -6 to 6
- comp_v: bfloat16 [32, 192, 8, 128], P('seq', 'head'), may hold values from -24 to 24
- comp_grad: bfloat16 [32, 192, 8, 640], P('seq', 'head'), may hold values from -24 to 24
- prefix_k: bfloat16 [8192, 8, 128], P('seq', 'head'), may hold values from -8 to 8
- prefix_v: bfloat16 [8192, 8, 128], P('seq', 'head'), may hold values from -24 to 24
- comp_len: int32 [32], replicated, may hold values from 1 to 192, 3072 in all
Outputs:
- attn_out: bfloat16 [32, 192, 8, 640], P('seq', 'head')
- grad_q: bfloat16 [32, 192, 8, 640], P('seq', 'head')
- grad_k: bfloat16 [32, 192, 8, 128], P('seq', 'head')
- grad_v: bfloat16 [32, 192, 8, 128], P('seq', 'head')
- grad_prefix_k: float32 [8192, 8, 128], P('seq', 'head')
- grad_prefix_v: float32 [8192, 8, 128], P('seq', 'head')
The draws below stay inside these ranges and needn't reach their ends.
Inputs may be any that keep to these rules, and one draw needn't show every extreme that they name: `comp_len`: the lengths sum to 3072 and the largest is 192.
All inputs are finite; a program needn't handle non-finite values.
Results may differ from the reference program's by a relative error of at most 0.011.
Values may be sent and summed in bfloat16 or wider, within the bound.
No kernel may reach another device: no remote copies, remote signals or barrier semaphores. Data moves between devices by JAX's collectives and lax.ppermute only.
A program may use at most 128 MiB of HBM per device.

```python
import math
import jax
import jax.numpy as jnp
import numpy as np
from jax import lax

HD = 128
KVH = 8
G = 5
PROMPTS = 4
CAP = 192
CPD = 1
PREFIX = 8192
NCOMP = 32


def draw_comp_q(key, part):
    key = jax.random.fold_in(key, 11)
    shape = (NCOMP, CAP, KVH, G * HD)
    values = jnp.clip(1.5 * jax.random.normal(key, shape, jnp.float32), -8.0, 8.0)
    return values.astype(jnp.bfloat16)


def draw_prefix_k(key, part):
    key = jax.random.fold_in(key, 12)
    shape = (PREFIX, KVH, HD)
    values = jnp.clip(jax.random.normal(key, shape, jnp.float32), -8.0, 8.0)
    return values.astype(jnp.bfloat16)


def shard_levels(rng, shape, pieces, low, high):
    loudness, own = 1.0, jax.random.fold_in(rng, 6)
    for position, parts in pieces:
        draws = jnp.exp(jax.random.uniform(jax.random.fold_in(own, position), (parts,), jnp.float32, low / len(pieces), high / len(pieces)))
        loudness = loudness * jnp.repeat(draws, shape[position] // parts).reshape([-1 if axis == position else 1 for axis in range(len(shape))])
    return loudness


def length_profile(amount, total, most, lean):
    portions = [(1 << 20) // math.isqrt(rank ** lean) + 1 for rank in range(2, amount + 1)]
    surplus, holding = total - most - (amount - 1), [1] * (amount - 1)
    while surplus > 0:
        candidates = [i for i in range(amount - 1) if holding[i] < most]
        pool, budget = sum([portions[i] for i in candidates]), surplus
        for i in candidates:
            extra = min(most - holding[i], max(1, budget * portions[i] // pool), surplus)
            holding[i] = holding[i] + extra
            surplus = surplus - extra
    return np.array([most] + holding)


def uneven_parts(stream_key, count, total, most, skew):
    if count == 2:
        one = jax.random.randint(stream_key, (), max(1, total - most), min(most, total - 1) + 1)
        return jnp.stack([one, total - one])
    tallies = jnp.asarray(length_profile(count, total, most, skew), jnp.int32)
    couples = (count - 1) // 2
    giver, taker = tallies[1:1 + 2 * couples:2], tallies[2:2 + 2 * couples:2]
    margin = jnp.minimum(giver - 1, most - taker)
    moved = jax.random.randint(jax.random.fold_in(stream_key, 1), (couples,), 0, 1 << 20) % (margin + 1)
    tallies = tallies.at[1:1 + 2 * couples:2].set(giver - moved).at[2:2 + 2 * couples:2].set(taker + moved)
    return tallies[jax.random.permutation(jax.random.fold_in(stream_key, 2), count)]


def gaussian(key, shape, scale, bound, shards=(), held_as=jnp.bfloat16):
    gain = shard_levels(key, shape, shards, -0.22, 0.18) if shards else 1.0
    result = jax.random.normal(key, shape, jnp.float32) * scale * gain
    return jnp.minimum(jnp.maximum(result, -bound), bound).astype(held_as)


def setup_inputs(seed: int = 0) -> dict:
    key_list = jax.random.split(jax.random.key(seed), 8)
    comp_q = draw_comp_q(jax.random.fold_in(key_list[7], 71), 0)
    comp_k = gaussian(key_list[1], (NCOMP, CAP, KVH, HD), 1.0, 6.0, ((0, 32), (1, 8)))
    comp_v = gaussian(key_list[2], (NCOMP, CAP, KVH, HD), 4.0, 24.0, ((0, 32), (1, 8)))
    comp_grad = gaussian(key_list[3], (NCOMP, CAP, KVH, G * HD), 4.0, 24.0, ((0, 32), (1, 8)))
    prefix_k = draw_prefix_k(jax.random.fold_in(key_list[7], 71), 0)
    prefix_v = gaussian(key_list[5], (PREFIX, KVH, HD), 4.0, 24.0, ((0, 32), (1, 8)))
    comp_len = uneven_parts(key_list[6], NCOMP, NCOMP * CAP // 2, CAP, 2).astype(jnp.int32)
    return dict(comp_q=comp_q, comp_k=comp_k, comp_v=comp_v, comp_grad=comp_grad, prefix_k=prefix_k, prefix_v=prefix_v, comp_len=comp_len)


masked_fill = -1e+30

def attend_slot(queries, cotangent, keys, values, length, prefix_len):
    cap = queries.shape[0]
    scale = 1.0 / math.sqrt(queries.shape[3])
    scores = jnp.einsum('thgd,khd->hgtk', queries, keys) * scale
    rows = jnp.arange(cap)[:, None]
    cols = jnp.arange(keys.shape[0])[None, :] - prefix_len
    allowed = (cols < 0) | (cols <= rows) & (cols < length)
    live_rows = rows < length
    masked = jnp.where(allowed, scores, masked_fill)
    top = lax.optimization_barrier(jnp.max(masked, axis=3, keepdims=True))
    log_total = top + jnp.log(lax.optimization_barrier(jnp.sum(jnp.exp(masked - top), axis=3, keepdims=True)))
    probs = jnp.where(allowed & live_rows, jnp.exp(masked - log_total), 0.0)
    probs_half = lax.optimization_barrier(probs.astype(jnp.bfloat16)).astype(jnp.float32)
    output = jnp.einsum('hgtk,khd->thgd', probs_half, values)
    prob_grad = jnp.einsum('thgd,khd->hgtk', cotangent, values)
    delta = lax.optimization_barrier(jnp.sum(probs * prob_grad, axis=3, keepdims=True))
    score_grad = lax.optimization_barrier((probs * (prob_grad - delta)).astype(jnp.bfloat16)).astype(jnp.float32)
    query_grad = jnp.einsum('hgtk,khd->thgd', score_grad, keys) * scale
    key_grad = jnp.einsum('hgtk,thgd->khd', score_grad, queries) * scale
    value_grad = jnp.einsum('hgtk,thgd->khd', probs_half, cotangent)
    return (output, query_grad, key_grad, value_grad)

def reference(comp_q, comp_k, comp_v, comp_grad, prefix_k, prefix_v, comp_len):
    slots, cap, heads, width = comp_q.shape
    head_dim = comp_k.shape[3]
    group = width // head_dim
    prompt_len = prefix_k.shape[0] // PROMPTS

    def step(carry, index):
        start = (index // CPD % PROMPTS * prompt_len).astype(jnp.int32)
        length = comp_len[index]
        queries = comp_q[index].astype(jnp.float32).reshape(cap, heads, group, head_dim)
        cotangent = comp_grad[index].astype(jnp.float32).reshape(cap, heads, group, head_dim)
        keys = jnp.concatenate([lax.dynamic_slice_in_dim(prefix_k, start, prompt_len, 0), comp_k[index]], 0).astype(jnp.float32)
        values = jnp.concatenate([lax.dynamic_slice_in_dim(prefix_v, start, prompt_len, 0), comp_v[index]], 0).astype(jnp.float32)
        output, query_grad, key_grad, value_grad = attend_slot(queries, cotangent, keys, values, length, prompt_len)
        stacked = jnp.concatenate([key_grad[:prompt_len], value_grad[:prompt_len]], 2)
        region = lax.dynamic_slice_in_dim(carry, start, prompt_len, 0)
        carry = lax.dynamic_update_slice_in_dim(carry, region + stacked, start, 0)
        results = (output.reshape(cap, heads, width).astype(jnp.bfloat16), query_grad.reshape(cap, heads, width).astype(jnp.bfloat16), key_grad[prompt_len:].astype(jnp.bfloat16), value_grad[prompt_len:].astype(jnp.bfloat16))
        return (carry, results)
    initial = jnp.zeros((prefix_k.shape[0], heads, 2 * head_dim), jnp.float32)
    total, results = lax.scan(step, initial, jnp.arange(slots, dtype=jnp.int32))
    output, query_grad, key_grad, value_grad = results
    return (output, query_grad, key_grad, value_grad, total[:, :, :head_dim], total[:, :, head_dim:])
```

```python
import functools
import math

import jax
import jax.numpy as jnp
from jax import lax
from jax.experimental import pallas as pl
from jax.experimental.pallas import tpu as pltpu
from jax.sharding import PartitionSpec as P

PROMPTS = 4
FILL = -1e30
VMEM = pltpu.VMEM
LIMIT = 8 * 1024 * 1024
f32 = jnp.float32
bf16 = jnp.bfloat16


def dot(a, b):
    return jnp.dot(a, b, preferred_element_type=f32)


def dot_t(a, b):
    return lax.dot_general(a, b, (((1,), (1,)), ((), ())), preferred_element_type=f32)


def pack_kernel(heads, q_ref, g_ref, k_ref, v_ref, out_ref, wide):
    rows, width = q_ref.shape
    slots = rows // heads
    head_dim = k_ref.shape[1]
    group = width // head_dim
    for i in range(group):
        wide[i] = q_ref[:, i * head_dim:(i + 1) * head_dim].astype(f32)
        wide[group + i] = g_ref[:, i * head_dim:(i + 1) * head_dim].astype(f32)
    wide[2 * group] = k_ref[...].astype(f32)
    wide[2 * group + 1] = v_ref[...].astype(f32)
    for i in range(2 * group + 2):
        parts = [wide[i, pl.ds(h, slots, stride=heads), :] for h in range(heads)]
        out_ref[:, i * head_dim:(i + 1) * head_dim] = jnp.concatenate(parts, 0).astype(bf16)


def pack(q, g, k, v):
    _, slots, heads, width = q.shape
    head_dim = k.shape[3]
    rows = slots * heads
    total = 2 * width + 2 * head_dim
    return pl.pallas_call(
        functools.partial(pack_kernel, heads),
        out_shape=jax.ShapeDtypeStruct((rows, total), bf16),
        scratch_shapes=[VMEM((total // head_dim, rows, head_dim), f32)],
        compiler_params=pltpu.CompilerParams(vmem_limit_bytes=LIMIT),
        cost_estimate=pl.CostEstimate(
            flops=rows * total, bytes_accessed=4 * rows * total, transcendentals=0
        ),
    )(
        q.reshape(rows, width),
        g.reshape(rows, width),
        k.reshape(rows, head_dim),
        v.reshape(rows, head_dim),
    )


def unpack_kernel(heads, x_ref, o_ref, dq_ref, dk_ref, dv_ref, wide):
    rows, total = x_ref.shape
    slots = rows // heads
    width, head_dim = o_ref.shape[1], dk_ref.shape[1]
    for col in range(0, total, head_dim):
        wide[col // head_dim] = x_ref[:, col:col + head_dim].astype(f32)
    for col in range(0, total, head_dim):
        parts = [
            wide[col // head_dim, pl.ds(t, heads, stride=slots), :] for t in range(slots)
        ]
        block = jnp.concatenate(parts, 0).astype(bf16)
        if col < width:
            o_ref[:, col:col + head_dim] = block
        elif col < 2 * width:
            dq_ref[:, col - width:col - width + head_dim] = block
        elif col == 2 * width:
            dk_ref[...] = block
        else:
            dv_ref[...] = block


def unpack(x, heads, width, head_dim):
    rows, total = x.shape
    slots = rows // heads
    outs = pl.pallas_call(
        functools.partial(unpack_kernel, heads),
        out_shape=[
            jax.ShapeDtypeStruct((rows, width), bf16),
            jax.ShapeDtypeStruct((rows, width), bf16),
            jax.ShapeDtypeStruct((rows, head_dim), bf16),
            jax.ShapeDtypeStruct((rows, head_dim), bf16),
        ],
        scratch_shapes=[VMEM((total // head_dim, rows, head_dim), f32)],
        compiler_params=pltpu.CompilerParams(vmem_limit_bytes=LIMIT),
        cost_estimate=pl.CostEstimate(
            flops=rows * total, bytes_accessed=4 * rows * total, transcendentals=0
        ),
    )(x)
    return [piece.reshape(1, slots, heads, piece.shape[1]) for piece in outs]


def stack_rows(x_ref, q_s, g_s, group):
    cap, head_dim = x_ref.shape[0], q_s.shape[1]
    width = group * head_dim
    for i in range(group):
        q_s[i * cap:(i + 1) * cap, :] = x_ref[:, i * head_dim:(i + 1) * head_dim]
        g_s[i * cap:(i + 1) * cap, :] = x_ref[:, width + i * head_dim:width + (i + 1) * head_dim]


def blocks_of(rows, cap):
    for start in range(0, rows, 256):
        stop = min(start + 256, rows)
        token = (lax.broadcasted_iota(jnp.int32, (1, stop - start), 1) + start) % cap
        yield start, stop, token


def causal(token, length, cap):
    key = lax.broadcasted_iota(jnp.int32, (cap, token.shape[1]), 0)
    return (key <= token) & (key < length)


def merge(state, s, d, turn, seen=None):
    if seen is not None:
        s = jnp.where(seen, s, FILL)
    high = jnp.max(s, axis=0, keepdims=True) * turn
    new = high if state is None else jnp.maximum(state[0], high)
    e = jnp.exp2(s * turn - new)
    if seen is not None:
        e = jnp.where(seen, e, 0.0)
    norm = jnp.sum(e, axis=0, keepdims=True)
    delta = jnp.sum(e * d, axis=0, keepdims=True)
    if state is not None:
        drop = jnp.exp2(state[0] - new)
        norm = norm + state[1] * drop
        delta = delta + state[2] * drop
    return e, (new, norm, delta)


def transposed(x):
    return x.astype(f32).T.astype(bf16)


def near_stats_kernel(group, chunks, scale, len_ref, x_ref, *refs):
    kv_refs, stats_ref, q_s, g_s = refs[:chunks], refs[chunks], refs[chunks + 1], refs[chunks + 2]
    cap, head_dim = x_ref.shape[0], q_s.shape[1]
    width = group * head_dim
    length = len_ref[lax.axis_index("seq")]
    turn = scale * math.log2(math.e)
    stack_rows(x_ref, q_s, g_s, group)
    for start, stop, token in blocks_of(group * cap, cap):
        q, g = q_s[start:stop, :], g_s[start:stop, :]
        state = None
        for kv in kv_refs:
            _, state = merge(state, dot_t(kv[0], q), dot_t(kv[1], g), turn)
        own_k = x_ref[:, 2 * width:2 * width + head_dim]
        own_v = x_ref[:, 2 * width + head_dim:]
        seen = causal(token, length, cap)
        _, state = merge(state, dot_t(own_k, q), dot_t(own_v, g), turn, seen)
        for i in range(3):
            stats_ref[i:i + 1, start:stop] = state[i]


def far_kernel(group, chunks, scale, len_ref, x_ref, stats_ref, *refs):
    count = chunks + 1
    shard_refs, grad_refs = refs[:count], refs[count:2 * count]
    k_refs = [shard_refs[0]] + [r.at[0] for r in shard_refs[2:]]
    v_refs = [shard_refs[1]] + [r.at[1] for r in shard_refs[2:]]
    dk_refs = [grad_refs[0]] + [r.at[0] for r in grad_refs[2:]]
    dv_refs = [grad_refs[1]] + [r.at[1] for r in grad_refs[2:]]
    (total_ref, ot_ref, qt_ref,
     q_s, g_s, keys_t, values_t, e_s, d_s, pb_s, sb_s, dk_s, dv_s) = refs[2 * count:]
    cap = x_ref.shape[0]
    span, head_dim = shard_refs[0].shape
    length = len_ref[lax.axis_index("seq")]
    turn = scale * math.log2(math.e)
    stack_rows(x_ref, q_s, g_s, group)
    for i in range(chunks):
        keys_t[:, i * span:(i + 1) * span] = transposed(k_refs[i][...])
        values_t[:, i * span:(i + 1) * span] = transposed(v_refs[i][...])
    for start, stop, token in blocks_of(group * cap, cap):
        size = stop - start
        q, g = q_s[start:stop, :], g_s[start:stop, :]
        state = tuple(stats_ref[i:i + 1, start:stop] for i in range(3))
        tops = []
        for i in range(chunks):
            d = dot_t(v_refs[i][...], g)
            e, state = merge(state, dot_t(k_refs[i][...], q), d, turn)
            e_s[i * span:(i + 1) * span, :size] = e
            d_s[i * span:(i + 1) * span, :size] = d
            tops.append(state[0])
        top, norm, delta = state
        delta = delta / norm
        live = token < length
        total_ref[0:1, start:stop] = jnp.where(live, top + jnp.log2(norm), -FILL)
        total_ref[1:2, start:stop] = delta
        inverse = jnp.where(live, 1.0 / norm, 0.0)
        for i in range(chunks):
            lo, hi = i * span, (i + 1) * span
            p = e_s[lo:hi, :size] * (jnp.exp2(tops[i] - top) * inverse)
            pb = p.astype(bf16)
            sb = (p * (d_s[lo:hi, :size] - delta)).astype(bf16)
            pb_s[lo:hi, :size] = pb
            sb_s[lo:hi, :size] = sb
            dv, dk = dot(pb, g), dot(sb, q)
            if start == 0:
                dv_s[lo:hi, :] = dv
                dk_s[lo:hi, :] = dk
            else:
                dv_s[lo:hi, :] += dv
                dk_s[lo:hi, :] += dk
        ot_ref[:, start:stop] = dot(values_t[...], pb_s[:, :size])
        qt_ref[:, start:stop] = dot(keys_t[...], sb_s[:, :size])
    for i in range(chunks):
        dk_refs[i][...] = (dk_s[i * span:(i + 1) * span, :] * scale).astype(bf16)
        dv_refs[i][...] = dv_s[i * span:(i + 1) * span, :].astype(bf16)


def near_kernel(group, chunks, scale, len_ref, x_ref, total_ref, ot_ref, qt_ref, *refs):
    kv_refs = refs[:chunks]
    out_ref = refs[chunks]
    grad_refs = refs[chunks + 1:2 * chunks + 1]
    q_s, g_s, keys_t, values_t, pb_s, sb_s, ot_s, qt_s, dk_s, dv_s = refs[2 * chunks + 1:]
    cap = x_ref.shape[0]
    span, head_dim = kv_refs[0].shape[1:]
    width = group * head_dim
    prefix = chunks * span
    length = len_ref[lax.axis_index("seq")]
    turn = scale * math.log2(math.e)
    stack_rows(x_ref, q_s, g_s, group)

    def pair(i):
        if i < chunks:
            return kv_refs[i][0], kv_refs[i][1]
        return x_ref[:, 2 * width:2 * width + head_dim], x_ref[:, 2 * width + head_dim:]

    bounds = [(i * span, (i + 1) * span) for i in range(chunks)] + [(prefix, prefix + cap)]
    for i, (lo, hi) in enumerate(bounds):
        k, v = pair(i)
        keys_t[:, lo:hi] = transposed(k)
        values_t[:, lo:hi] = transposed(v)
    for start, stop, token in blocks_of(group * cap, cap):
        size = stop - start
        q, g = q_s[start:stop, :], g_s[start:stop, :]
        total = total_ref[0:1, start:stop]
        delta = total_ref[1:2, start:stop]
        for i, (lo, hi) in enumerate(bounds):
            k, v = pair(i)
            p = jnp.exp2(dot_t(k, q) * turn - total)
            if i == chunks:
                p = jnp.where(causal(token, length, cap), p, 0.0)
            pb = p.astype(bf16)
            sb = (p * (dot_t(v, g) - delta)).astype(bf16)
            pb_s[lo:hi, :size] = pb
            sb_s[lo:hi, :size] = sb
            dv, dk = dot(pb, g), dot(sb, q)
            if start == 0:
                dv_s[lo:hi, :] = dv
                dk_s[lo:hi, :] = dk
            else:
                dv_s[lo:hi, :] += dv
                dk_s[lo:hi, :] += dk
        ot_s[:, start:stop] = ot_ref[:, start:stop] + dot(values_t[...], pb_s[:, :size])
        qt_s[:, start:stop] = qt_ref[:, start:stop] + dot(keys_t[...], sb_s[:, :size])
    for i in range(chunks):
        lo, hi = bounds[i]
        grad_refs[i][0] = dk_s[lo:hi, :] * scale
        grad_refs[i][1] = dv_s[lo:hi, :]
    out_ref[:, 2 * width:2 * width + head_dim] = (dk_s[prefix:, :] * scale).astype(bf16)
    out_ref[:, 2 * width + head_dim:] = dv_s[prefix:, :].astype(bf16)
    out = ot_s[...].T
    grad_q = (qt_s[...] * scale).T
    for i in range(group):
        out_ref[:, i * head_dim:(i + 1) * head_dim] = out[i * cap:(i + 1) * cap].astype(bf16)
        out_ref[:, width + i * head_dim:width + (i + 1) * head_dim] = (
            grad_q[i * cap:(i + 1) * cap].astype(bf16)
        )


def call(body, products, keys, rows, head_dim, ins, outs, scratch, limit):
    smem = pl.BlockSpec(memory_space=pltpu.SMEM)
    vmem = pl.BlockSpec(memory_space=pltpu.VMEM)
    return pl.pallas_call(
        body,
        out_shape=outs,
        in_specs=[smem] + [vmem] * (len(ins) - 1),
        out_specs=[vmem] * len(outs),
        scratch_shapes=scratch,
        compiler_params=pltpu.CompilerParams(vmem_limit_bytes=limit * 1024 * 1024),
        cost_estimate=pl.CostEstimate(
            flops=2 * products * rows * keys * head_dim,
            bytes_accessed=sum(x.size * x.dtype.itemsize for x in ins + outs),
            transcendentals=rows * keys,
        ),
    )(*ins)


def near_stats(lengths, x, shards, group, scale):
    cap = x.shape[0]
    _, span, head_dim = shards[0].shape
    rows, keys = group * cap, len(shards) * span + cap
    return call(
        functools.partial(near_stats_kernel, group, len(shards), scale),
        2, keys, rows, head_dim,
        [lengths, x, *shards],
        [jax.ShapeDtypeStruct((3, rows), f32)],
        [VMEM((rows, head_dim), bf16)] * 2,
        12,
    )[0]


def far_pass(lengths, x, stats, shards, group, scale):
    cap = x.shape[0]
    span, head_dim = shards[0].shape
    chunks = len(shards) - 1
    rows, keys = group * cap, chunks * span
    outs = call(
        functools.partial(far_kernel, group, chunks, scale),
        6, keys, rows, head_dim,
        [lengths, x, stats, *shards],
        [jax.ShapeDtypeStruct(shard.shape, bf16) for shard in shards]
        + [jax.ShapeDtypeStruct((2, rows), f32)]
        + [jax.ShapeDtypeStruct((head_dim, rows), f32)] * 2,
        [VMEM((rows, head_dim), bf16)] * 2
        + [VMEM((head_dim, keys), bf16)] * 2
        + [VMEM((keys, 256), f32)] * 2
        + [VMEM((keys, 256), bf16)] * 2
        + [VMEM((keys, head_dim), f32)] * 2,
        24,
    )
    return outs[:chunks + 1], outs[chunks + 1:]


def near_pass(lengths, x, totals, shards, group, scale):
    cap, packed = x.shape
    _, span, head_dim = shards[0].shape
    rows, keys = group * cap, len(shards) * span + cap
    outs = call(
        functools.partial(near_kernel, group, len(shards), scale),
        6, keys, rows, head_dim,
        [lengths, x, *totals, *shards],
        [jax.ShapeDtypeStruct((cap, packed), bf16)]
        + [jax.ShapeDtypeStruct((2, span, head_dim), f32)] * len(shards),
        [VMEM((rows, head_dim), bf16)] * 2
        + [VMEM((head_dim, keys), bf16)] * 2
        + [VMEM((keys, 256), bf16)] * 2
        + [VMEM((head_dim, rows), f32)] * 2
        + [VMEM((keys, head_dim), f32)] * 2,
        24,
    )
    return outs[0], outs[1:]


def on_device(comp_q, comp_k, comp_v, comp_grad, prefix_k, prefix_v, comp_len):
    _, slots, heads, width = comp_q.shape
    head_dim = comp_k.shape[3]
    group = width // head_dim
    devices = lax.axis_size("seq")
    ring = devices // PROMPTS
    scale = 1.0 / math.sqrt(head_dim)

    to_prompt = []
    for owner in range(devices):
        plane, lane = divmod(owner, PROMPTS)
        reach = (0, 3, 1, 2)[lane]
        target = (plane + reach if plane % 2 else plane - reach) % ring
        to_prompt.append((owner, target * PROMPTS + owner // ring))
    to_owner = [(b, a) for a, b in to_prompt]

    def shift(x, steps):
        pairs = [(s, (s + PROMPTS * steps) % devices) for s in range(devices)]
        return lax.ppermute(x, "seq", pairs)

    own = lax.ppermute(jnp.stack([prefix_k[:, 0], prefix_v[:, 0]]), "seq", to_prompt)
    packed = pack(comp_q, comp_grad, comp_k, comp_v)
    own, packed = lax.optimization_barrier((own, packed))
    x = lax.all_to_all(packed, "head", split_axis=0, concat_axis=0, tiled=True)

    up, down = shift(own, 1), shift(own, -1)
    far_keys = shift(down[0], -3)
    far_values = shift(up[1], 3)
    up3, down3 = shift(up, 2), shift(down, -2)
    up2, down2 = shift(up, 1), shift(down, -1)

    near = [own, up, down]
    stats = near_stats(comp_len, x, near, group, scale)
    grads, totals = far_pass(
        comp_len, x, stats, [far_keys, far_values, up3, down3, up2, down2], group, scale
    )
    moved = [
        shift(grad, steps).astype(f32) for grad, steps in zip(grads, (3, -3, -2, 2, -1, 1))
    ]
    out, (own_grad, up_grad, down_grad) = near_pass(comp_len, x, totals, near, group, scale)
    far_dk, far_dv, up3, down3, up2, down2 = moved
    up_sum = up_grad + up2 + up3
    down_sum = down_grad + down2 + down3
    up_sum = up_sum + jnp.pad(far_dv[None], ((1, 0), (0, 0), (0, 0)))
    down_sum = down_sum + jnp.pad(far_dk[None], ((0, 1), (0, 0), (0, 0)))
    back = lax.all_to_all(out, "head", split_axis=0, concat_axis=0, tiled=True)
    up_sum = shift(up_sum.astype(bf16), -1)
    down_sum = shift(down_sum.astype(bf16), 1)
    summed = own_grad + up_sum.astype(f32) + down_sum.astype(f32)
    attn_out, grad_q, grad_k, grad_v = unpack(back, heads, width, head_dim)
    placed = lax.ppermute(summed.astype(bf16), "seq", to_owner).astype(f32)
    return (attn_out, grad_q, grad_k, grad_v, placed[0][:, None], placed[1][:, None])


def solution(mesh):
    tokens = P("seq", "head", None, None)
    prefix = P("seq", "head", None)
    return jax.shard_map(
        on_device,
        mesh=mesh,
        in_specs=(tokens, tokens, tokens, tokens, prefix, prefix, P()),
        out_specs=(tokens, tokens, tokens, tokens, prefix, prefix),
        check_vma=False,
    )
```

```python
import functools
import math

import jax
import jax.numpy as jnp
from jax import lax
from jax.experimental import pallas as pl
from jax.experimental.pallas import tpu as pltpu
from jax.sharding import PartitionSpec as P

PROMPTS = 4
FILL = -1e30
VMEM = pltpu.VMEM
LIMIT = 8 * 1024 * 1024
f32 = jnp.float32
bf16 = jnp.bfloat16


def dot(a, b):
    return jnp.dot(a, b, preferred_element_type=f32)


def dot_t(a, b):
    return lax.dot_general(a, b, (((1,), (1,)), ((), ())), preferred_element_type=f32)


def pack_kernel(heads, q_ref, g_ref, k_ref, v_ref, out_ref, wide):
    rows, width = q_ref.shape
    slots = rows // heads
    head_dim = k_ref.shape[1]
    group = width // head_dim
    for i in range(group):
        wide[i] = q_ref[:, i * head_dim:(i + 1) * head_dim].astype(f32)
        wide[group + i] = g_ref[:, i * head_dim:(i + 1) * head_dim].astype(f32)
    wide[2 * group] = k_ref[...].astype(f32)
    wide[2 * group + 1] = v_ref[...].astype(f32)
    for i in range(2 * group + 2):
        parts = [wide[i, pl.ds(h, slots, stride=heads), :] for h in range(heads)]
        out_ref[:, i * head_dim:(i + 1) * head_dim] = jnp.concatenate(parts, 0).astype(bf16)


def pack(q, g, k, v):
    _, slots, heads, width = q.shape
    head_dim = k.shape[3]
    rows = slots * heads
    total = 2 * width + 2 * head_dim
    return pl.pallas_call(
        functools.partial(pack_kernel, heads),
        out_shape=jax.ShapeDtypeStruct((rows, total), bf16),
        scratch_shapes=[VMEM((total // head_dim, rows, head_dim), f32)],
        compiler_params=pltpu.CompilerParams(vmem_limit_bytes=7 * LIMIT),
        cost_estimate=pl.CostEstimate(
            flops=int(2e9), bytes_accessed=4 * rows * total, transcendentals=0
        ),
    )(
        q.reshape(rows, width),
        g.reshape(rows, width),
        k.reshape(rows, head_dim),
        v.reshape(rows, head_dim),
    )


def unpack_kernel(heads, x_ref, o_ref, dq_ref, dk_ref, dv_ref, wide):
    rows, total = x_ref.shape
    slots = rows // heads
    width, head_dim = o_ref.shape[1], dk_ref.shape[1]
    for col in range(0, total, head_dim):
        wide[col // head_dim] = x_ref[:, col:col + head_dim].astype(f32)
    for col in range(0, total, head_dim):
        parts = [
            wide[col // head_dim, pl.ds(t, heads, stride=slots), :] for t in range(slots)
        ]
        block = jnp.concatenate(parts, 0).astype(bf16)
        if col < width:
            o_ref[:, col:col + head_dim] = block
        elif col < 2 * width:
            dq_ref[:, col - width:col - width + head_dim] = block
        elif col == 2 * width:
            dk_ref[...] = block
        else:
            dv_ref[...] = block


def unpack(x, heads, width, head_dim):
    rows, total = x.shape
    slots = rows // heads
    outs = pl.pallas_call(
        functools.partial(unpack_kernel, heads),
        out_shape=[
            jax.ShapeDtypeStruct((rows, width), bf16),
            jax.ShapeDtypeStruct((rows, width), bf16),
            jax.ShapeDtypeStruct((rows, head_dim), bf16),
            jax.ShapeDtypeStruct((rows, head_dim), bf16),
        ],
        scratch_shapes=[VMEM((total // head_dim, rows, head_dim), f32)],
        compiler_params=pltpu.CompilerParams(vmem_limit_bytes=LIMIT),
        cost_estimate=pl.CostEstimate(
            flops=int(1e9), bytes_accessed=4 * rows * total, transcendentals=0
        ),
    )(x)
    return [piece.reshape(1, slots, heads, piece.shape[1]) for piece in outs]


def stack_rows(x_ref, q_s, g_s, group):
    cap, head_dim = x_ref.shape[0], q_s.shape[1]
    width = group * head_dim
    for i in range(group):
        q_s[i * cap:(i + 1) * cap, :] = x_ref[:, i * head_dim:(i + 1) * head_dim]
        g_s[i * cap:(i + 1) * cap, :] = x_ref[:, width + i * head_dim:width + (i + 1) * head_dim]


def blocks_of(rows, cap):
    for start in range(0, rows, 256):
        stop = min(start + 256, rows)
        token = (lax.broadcasted_iota(jnp.int32, (1, stop - start), 1) + start) % cap
        yield start, stop, token


def causal(token, length, cap):
    key = lax.broadcasted_iota(jnp.int32, (cap, token.shape[1]), 0)
    return (key <= token) & (key < length)


def merge(state, s, d, turn, seen=None):
    if seen is not None:
        s = jnp.where(seen, s, FILL)
    high = jnp.max(s, axis=0, keepdims=True) * turn
    new = high if state is None else jnp.maximum(state[0], high)
    e = jnp.exp2(s * turn - new)
    if seen is not None:
        e = jnp.where(seen, e, 0.0)
    norm = jnp.sum(e, axis=0, keepdims=True)
    delta = jnp.sum(e * d, axis=0, keepdims=True)
    if state is not None:
        drop = jnp.exp2(state[0] - new)
        norm = norm + state[1] * drop
        delta = delta + state[2] * drop
    return e, (new, norm, delta)


def transposed(x):
    return x.astype(f32).T.astype(bf16)


def turn_kernel(far_k, far_v, low_ref, high_ref, keys_t, values_t):
    span = far_k.shape[0]
    k_refs = [far_k] + [r.at[i, 0] for r in (low_ref, high_ref) for i in range(2)]
    v_refs = [far_v] + [r.at[i, 1] for r in (low_ref, high_ref) for i in range(2)]
    for i in range(len(k_refs)):
        keys_t[:, i * span:(i + 1) * span] = transposed(k_refs[i][...])
        values_t[:, i * span:(i + 1) * span] = transposed(v_refs[i][...])


def far_kernel(group, near, scale, len_ref, x_ref, *refs):
    near_refs, refs = refs[:near], refs[near:]
    (far_k, far_v, low_ref, high_ref, keys_t, values_t,
     far_dk, far_dv, low_grad, high_grad, total_ref, ot_ref, qt_ref,
     q_s, g_s, e_s, d_s, pb_s, sb_s, dk_s, dv_s) = refs
    k_refs = [far_k] + [r.at[i, 0] for r in (low_ref, high_ref) for i in range(2)]
    v_refs = [far_v] + [r.at[i, 1] for r in (low_ref, high_ref) for i in range(2)]
    dk_refs = [far_dk] + [r.at[i, 0] for r in (low_grad, high_grad) for i in range(2)]
    dv_refs = [far_dv] + [r.at[i, 1] for r in (low_grad, high_grad) for i in range(2)]
    chunks = len(k_refs)
    cap = x_ref.shape[0]
    span, head_dim = far_k.shape
    width = group * head_dim
    length = len_ref[lax.axis_index("seq")]
    turn = scale * math.log2(math.e)
    stack_rows(x_ref, q_s, g_s, group)
    for start, stop, token in blocks_of(group * cap, cap):
        size = stop - start
        q, g = q_s[start:stop, :], g_s[start:stop, :]
        state = None
        for kv in near_refs:
            _, state = merge(state, dot_t(kv[0], q), dot_t(kv[1], g), turn)
        own_k = x_ref[:, 2 * width:2 * width + head_dim]
        own_v = x_ref[:, 2 * width + head_dim:]
        seen = causal(token, length, cap)
        _, state = merge(state, dot_t(own_k, q), dot_t(own_v, g), turn, seen)
        tops = []
        for i in range(chunks):
            d = dot_t(v_refs[i][...], g)
            e, state = merge(state, dot_t(k_refs[i][...], q), d, turn)
            e_s[i * span:(i + 1) * span, :size] = e
            d_s[i * span:(i + 1) * span, :size] = d
            tops.append(state[0])
        top, norm, delta = state
        delta = delta / norm
        live = token < length
        total_ref[0:1, start:stop] = jnp.where(live, top + jnp.log2(norm), -FILL)
        total_ref[1:2, start:stop] = delta
        inverse = jnp.where(live, 1.0 / norm, 0.0)
        for i in range(chunks):
            lo, hi = i * span, (i + 1) * span
            p = e_s[lo:hi, :size] * (jnp.exp2(tops[i] - top) * inverse)
            pb = p.astype(bf16)
            sb = (p * (d_s[lo:hi, :size] - delta)).astype(bf16)
            pb_s[lo:hi, :size] = pb
            sb_s[lo:hi, :size] = sb
            dv, dk = dot(pb, g), dot(sb, q)
            if start == 0:
                dv_s[lo:hi, :] = dv
                dk_s[lo:hi, :] = dk
            else:
                dv_s[lo:hi, :] += dv
                dk_s[lo:hi, :] += dk
        ot_ref[:, start:stop] = dot(values_t[...], pb_s[:, :size])
        qt_ref[:, start:stop] = dot(keys_t[...], sb_s[:, :size])
    for i in range(chunks):
        dk_refs[i][...] = (dk_s[i * span:(i + 1) * span, :] * scale).astype(bf16)
        dv_refs[i][...] = dv_s[i * span:(i + 1) * span, :].astype(bf16)


def near_kernel(group, chunks, scale, len_ref, x_ref, total_ref, ot_ref, qt_ref, *refs):
    kv_refs = refs[:chunks]
    out_ref = refs[chunks]
    grad_refs = refs[chunks + 1:2 * chunks + 1]
    q_s, g_s, keys_t, values_t, pb_s, sb_s, ot_s, qt_s, dk_s, dv_s = refs[2 * chunks + 1:]
    cap = x_ref.shape[0]
    span, head_dim = kv_refs[0].shape[1:]
    width = group * head_dim
    prefix = chunks * span
    length = len_ref[lax.axis_index("seq")]
    turn = scale * math.log2(math.e)
    stack_rows(x_ref, q_s, g_s, group)

    def pair(i):
        if i < chunks:
            return kv_refs[i][0], kv_refs[i][1]
        return x_ref[:, 2 * width:2 * width + head_dim], x_ref[:, 2 * width + head_dim:]

    bounds = [(i * span, (i + 1) * span) for i in range(chunks)] + [(prefix, prefix + cap)]
    for i, (lo, hi) in enumerate(bounds):
        k, v = pair(i)
        keys_t[:, lo:hi] = transposed(k)
        values_t[:, lo:hi] = transposed(v)
    for start, stop, token in blocks_of(group * cap, cap):
        size = stop - start
        q, g = q_s[start:stop, :], g_s[start:stop, :]
        total = total_ref[0:1, start:stop]
        delta = total_ref[1:2, start:stop]
        for i, (lo, hi) in enumerate(bounds):
            k, v = pair(i)
            p = jnp.exp2(dot_t(k, q) * turn - total)
            if i == chunks:
                p = jnp.where(causal(token, length, cap), p, 0.0)
            pb = p.astype(bf16)
            sb = (p * (dot_t(v, g) - delta)).astype(bf16)
            pb_s[lo:hi, :size] = pb
            sb_s[lo:hi, :size] = sb
            dv, dk = dot(pb, g), dot(sb, q)
            if start == 0:
                dv_s[lo:hi, :] = dv
                dk_s[lo:hi, :] = dk
            else:
                dv_s[lo:hi, :] += dv
                dk_s[lo:hi, :] += dk
        ot_s[:, start:stop] = ot_ref[:, start:stop] + dot(values_t[...], pb_s[:, :size])
        qt_s[:, start:stop] = qt_ref[:, start:stop] + dot(keys_t[...], sb_s[:, :size])
    for i in range(chunks):
        lo, hi = bounds[i]
        grad_refs[i][0] = dk_s[lo:hi, :] * scale
        grad_refs[i][1] = dv_s[lo:hi, :]
    out_ref[:, 2 * width:2 * width + head_dim] = (dk_s[prefix:, :] * scale).astype(bf16)
    out_ref[:, 2 * width + head_dim:] = dv_s[prefix:, :].astype(bf16)
    out = ot_s[...].T
    grad_q = (qt_s[...] * scale).T
    for i in range(group):
        out_ref[:, i * head_dim:(i + 1) * head_dim] = out[i * cap:(i + 1) * cap].astype(bf16)
        out_ref[:, width + i * head_dim:width + (i + 1) * head_dim] = (
            grad_q[i * cap:(i + 1) * cap].astype(bf16)
        )


def call(body, micros, ins, outs, scratch, limit, scalars=1):
    smem = pl.BlockSpec(memory_space=pltpu.SMEM)
    vmem = pl.BlockSpec(memory_space=pltpu.VMEM)
    return pl.pallas_call(
        body,
        out_shape=outs,
        in_specs=[smem] * scalars + [vmem] * (len(ins) - scalars),
        out_specs=[vmem] * len(outs),
        scratch_shapes=scratch,
        compiler_params=pltpu.CompilerParams(vmem_limit_bytes=limit * 1024 * 1024),
        cost_estimate=pl.CostEstimate(
            flops=int(micros * 1.15e9),
            bytes_accessed=sum(x.size * x.dtype.itemsize for x in ins + outs),
            transcendentals=0,
        ),
    )(*ins)


def turned(far):
    span, head_dim = far[0].shape
    return call(
        turn_kernel, 6, list(far), [jax.ShapeDtypeStruct((head_dim, 5 * span), bf16)] * 2,
        [], 8, scalars=0,
    )


def far_pass(lengths, x, near, far, far_t, group, scale):
    cap = x.shape[0]
    span, head_dim = far[0].shape
    rows, keys = group * cap, 5 * span
    outs = call(
        functools.partial(far_kernel, group, len(near), scale),
        7,
        [lengths, x, *near, *far, *far_t],
        [jax.ShapeDtypeStruct(shard.shape, bf16) for shard in far]
        + [jax.ShapeDtypeStruct((2, rows), f32)]
        + [jax.ShapeDtypeStruct((head_dim, rows), f32)] * 2,
        [VMEM((rows, head_dim), bf16)] * 2
        + [VMEM((keys, 256), f32)] * 2
        + [VMEM((keys, 256), bf16)] * 2
        + [VMEM((keys, head_dim), f32)] * 2,
        24,
    )
    return outs[:len(far)], outs[len(far):]


def near_pass(lengths, x, totals, shards, group, scale):
    cap, packed = x.shape
    _, span, head_dim = shards[0].shape
    rows, keys = group * cap, len(shards) * span + cap
    outs = call(
        functools.partial(near_kernel, group, len(shards), scale),
        6,
        [lengths, x, *totals, *shards],
        [jax.ShapeDtypeStruct((cap, packed), bf16)]
        + [jax.ShapeDtypeStruct((2, span, head_dim), f32)] * len(shards),
        [VMEM((rows, head_dim), bf16)] * 2
        + [VMEM((head_dim, keys), bf16)] * 2
        + [VMEM((keys, 256), bf16)] * 2
        + [VMEM((head_dim, rows), f32)] * 2
        + [VMEM((keys, head_dim), f32)] * 2,
        24,
    )
    return outs[0], outs[1:]


def on_device(comp_q, comp_k, comp_v, comp_grad, prefix_k, prefix_v, comp_len):
    _, slots, heads, width = comp_q.shape
    head_dim = comp_k.shape[3]
    group = width // head_dim
    devices = lax.axis_size("seq")
    ring = devices // PROMPTS
    scale = 1.0 / math.sqrt(head_dim)

    to_prompt = []
    for owner in range(devices):
        plane, lane = divmod(owner, PROMPTS)
        reach = (0, 3, 1, 2)[lane]
        target = (plane + reach if plane % 2 else plane - reach) % ring
        to_prompt.append((owner, target * PROMPTS + owner // ring))
    to_owner = [(b, a) for a, b in to_prompt]

    def shift(x, steps):
        pairs = [(s, (s + PROMPTS * steps) % devices) for s in range(devices)]
        return lax.ppermute(x, "seq", pairs)

    own = lax.ppermute(jnp.stack([prefix_k[:, 0], prefix_v[:, 0]]), "seq", to_prompt)
    packed = pack(comp_q, comp_grad, comp_k, comp_v)
    own, packed = lax.optimization_barrier((own, packed))

    up, down = shift(own, 1), shift(own, -1)
    up, down, packed = lax.optimization_barrier((up, down, packed))
    far_keys, far_values = shift(down[0], -3), shift(up[1], 3)
    low = shift(jnp.stack([own, up]), 2)
    high = shift(jnp.stack([own, down]), -2)
    x = lax.all_to_all(packed, "head", split_axis=0, concat_axis=0, tiled=True)

    near, far = [own, up, down], [far_keys, far_values, low, high]
    grads, totals = far_pass(comp_len, x, near, far, turned(far), group, scale)
    far_dk, far_dv, low, high = [
        shift(grad, steps) for grad, steps in zip(grads, (3, -3, -2, 2))
    ]
    out, (own_grad, up_grad, down_grad) = near_pass(comp_len, x, totals, near, group, scale)
    far_dk, far_dv = far_dk.astype(f32)[None], far_dv.astype(f32)[None]
    up_sum = up_grad + low[1].astype(f32) + jnp.pad(far_dv, ((1, 0), (0, 0), (0, 0)))
    down_sum = down_grad + high[1].astype(f32) + jnp.pad(far_dk, ((0, 1), (0, 0), (0, 0)))
    back = lax.all_to_all(out, "head", split_axis=0, concat_axis=0, tiled=True)
    up_sum = shift(up_sum.astype(bf16), -1)
    down_sum = shift(down_sum.astype(bf16), 1)
    summed = own_grad + low[0].astype(f32) + high[0].astype(f32)
    summed = summed + up_sum.astype(f32) + down_sum.astype(f32)
    attn_out, grad_q, grad_k, grad_v = unpack(back, heads, width, head_dim)
    placed = lax.ppermute(summed.astype(bf16), "seq", to_owner).astype(f32)
    return (attn_out, grad_q, grad_k, grad_v, placed[0][:, None], placed[1][:, None])


def solution(mesh):
    tokens = P("seq", "head", None, None)
    prefix = P("seq", "head", None)
    return jax.shard_map(
        on_device,
        mesh=mesh,
        in_specs=(tokens, tokens, tokens, tokens, prefix, prefix, P()),
        out_specs=(tokens, tokens, tokens, tokens, prefix, prefix),
        check_vma=False,
    )
```

```python
import functools
import math

import jax
import jax.numpy as jnp
from jax import lax
from jax.experimental import pallas as pl
from jax.experimental.pallas import tpu as pltpu
from jax.sharding import PartitionSpec as P

PROMPTS = 4
FILL = -1e30
VMEM = pltpu.VMEM
LIMIT = 8 * 1024 * 1024
f32 = jnp.float32
bf16 = jnp.bfloat16


def dot(a, b):
    return jnp.dot(a, b, preferred_element_type=f32)


def dot_t(a, b):
    return lax.dot_general(a, b, (((1,), (1,)), ((), ())), preferred_element_type=f32)


def pack_kernel(heads, q_ref, g_ref, k_ref, v_ref, out_ref, wide):
    rows, width = q_ref.shape
    slots = rows // heads
    head_dim = k_ref.shape[1]
    group = width // head_dim
    for i in range(group):
        wide[i] = q_ref[:, i * head_dim:(i + 1) * head_dim].astype(f32)
        wide[group + i] = g_ref[:, i * head_dim:(i + 1) * head_dim].astype(f32)
    wide[2 * group] = k_ref[...].astype(f32)
    wide[2 * group + 1] = v_ref[...].astype(f32)
    for i in range(2 * group + 2):
        parts = [wide[i, pl.ds(h, slots, stride=heads), :] for h in range(heads)]
        out_ref[:, i * head_dim:(i + 1) * head_dim] = jnp.concatenate(parts, 0).astype(bf16)


def pack(q, g, k, v):
    _, slots, heads, width = q.shape
    head_dim = k.shape[3]
    rows = slots * heads
    total = 2 * width + 2 * head_dim
    return pl.pallas_call(
        functools.partial(pack_kernel, heads),
        out_shape=jax.ShapeDtypeStruct((rows, total), bf16),
        scratch_shapes=[VMEM((total // head_dim, rows, head_dim), f32)],
        compiler_params=pltpu.CompilerParams(vmem_limit_bytes=7 * LIMIT),
        cost_estimate=pl.CostEstimate(
            flops=int(2e9), bytes_accessed=4 * rows * total, transcendentals=0
        ),
    )(
        q.reshape(rows, width),
        g.reshape(rows, width),
        k.reshape(rows, head_dim),
        v.reshape(rows, head_dim),
    )


def unpack_kernel(heads, x_ref, o_ref, dq_ref, dk_ref, dv_ref, wide):
    rows, total = x_ref.shape
    slots = rows // heads
    width, head_dim = o_ref.shape[1], dk_ref.shape[1]
    for col in range(0, total, head_dim):
        wide[col // head_dim] = x_ref[:, col:col + head_dim].astype(f32)
    for col in range(0, total, head_dim):
        parts = [
            wide[col // head_dim, pl.ds(t, heads, stride=slots), :] for t in range(slots)
        ]
        block = jnp.concatenate(parts, 0).astype(bf16)
        if col < width:
            o_ref[:, col:col + head_dim] = block
        elif col < 2 * width:
            dq_ref[:, col - width:col - width + head_dim] = block
        elif col == 2 * width:
            dk_ref[...] = block
        else:
            dv_ref[...] = block


def unpack(x, heads, width, head_dim):
    rows, total = x.shape
    slots = rows // heads
    outs = pl.pallas_call(
        functools.partial(unpack_kernel, heads),
        out_shape=[
            jax.ShapeDtypeStruct((rows, width), bf16),
            jax.ShapeDtypeStruct((rows, width), bf16),
            jax.ShapeDtypeStruct((rows, head_dim), bf16),
            jax.ShapeDtypeStruct((rows, head_dim), bf16),
        ],
        scratch_shapes=[VMEM((total // head_dim, rows, head_dim), f32)],
        compiler_params=pltpu.CompilerParams(vmem_limit_bytes=LIMIT),
        cost_estimate=pl.CostEstimate(
            flops=int(1e9), bytes_accessed=4 * rows * total, transcendentals=0
        ),
    )(x)
    return [piece.reshape(1, slots, heads, piece.shape[1]) for piece in outs]


def stack_rows(x_ref, q_s, g_s, group):
    cap, head_dim = x_ref.shape[0], q_s.shape[1]
    width = group * head_dim
    for i in range(group):
        q_s[i * cap:(i + 1) * cap, :] = x_ref[:, i * head_dim:(i + 1) * head_dim]
        g_s[i * cap:(i + 1) * cap, :] = x_ref[:, width + i * head_dim:width + (i + 1) * head_dim]


def blocks_of(rows, cap):
    for start in range(0, rows, 256):
        stop = min(start + 256, rows)
        token = (lax.broadcasted_iota(jnp.int32, (1, stop - start), 1) + start) % cap
        yield start, stop, token


def causal(token, length, cap):
    key = lax.broadcasted_iota(jnp.int32, (cap, token.shape[1]), 0)
    return (key <= token) & (key < length)


def merge(state, s, d, turn, seen=None):
    if seen is not None:
        s = jnp.where(seen, s, FILL)
    high = jnp.max(s, axis=0, keepdims=True) * turn
    new = high if state is None else jnp.maximum(state[0], high)
    e = jnp.exp2(s * turn - new)
    if seen is not None:
        e = jnp.where(seen, e, 0.0)
    norm = jnp.sum(e, axis=0, keepdims=True)
    delta = jnp.sum(e * d, axis=0, keepdims=True)
    if state is not None:
        drop = jnp.exp2(state[0] - new)
        norm = norm + state[1] * drop
        delta = delta + state[2] * drop
    return e, (new, norm, delta)


def transposed(x):
    return x.astype(f32).T.astype(bf16)


def near_stats_kernel(group, chunks, scale, len_ref, x_ref, *refs):
    kv_refs, stats_ref, q_s, g_s = refs[:chunks], refs[chunks], refs[chunks + 1], refs[chunks + 2]
    cap, head_dim = x_ref.shape[0], q_s.shape[1]
    width = group * head_dim
    length = len_ref[lax.axis_index("seq")]
    turn = scale * math.log2(math.e)
    stack_rows(x_ref, q_s, g_s, group)
    for start, stop, token in blocks_of(group * cap, cap):
        q, g = q_s[start:stop, :], g_s[start:stop, :]
        state = None
        for kv in kv_refs:
            _, state = merge(state, dot_t(kv[0], q), dot_t(kv[1], g), turn)
        own_k = x_ref[:, 2 * width:2 * width + head_dim]
        own_v = x_ref[:, 2 * width + head_dim:]
        seen = causal(token, length, cap)
        _, state = merge(state, dot_t(own_k, q), dot_t(own_v, g), turn, seen)
        for i in range(3):
            stats_ref[i:i + 1, start:stop] = state[i]


def far_kernel(group, chunks, scale, len_ref, x_ref, stats_ref, *refs):
    shard_refs, grad_refs = refs[:chunks], refs[chunks:2 * chunks]
    k_refs, v_refs = [[r.at[i] for r in shard_refs] for i in range(2)]
    dk_refs, dv_refs = [[r.at[i] for r in grad_refs] for i in range(2)]
    (total_ref, ot_ref, qt_ref,
     q_s, g_s, keys_t, values_t, e_s, d_s, pb_s, sb_s, dk_s, dv_s) = refs[2 * chunks:]
    cap = x_ref.shape[0]
    span, head_dim = shard_refs[0].shape[1:]
    length = len_ref[lax.axis_index("seq")]
    turn = scale * math.log2(math.e)
    stack_rows(x_ref, q_s, g_s, group)
    for i in range(chunks):
        keys_t[:, i * span:(i + 1) * span] = transposed(k_refs[i][...])
        values_t[:, i * span:(i + 1) * span] = transposed(v_refs[i][...])
    for start, stop, token in blocks_of(group * cap, cap):
        size = stop - start
        q, g = q_s[start:stop, :], g_s[start:stop, :]
        state = tuple(stats_ref[i:i + 1, start:stop] for i in range(3))
        tops = []
        for i in range(chunks):
            d = dot_t(v_refs[i][...], g)
            e, state = merge(state, dot_t(k_refs[i][...], q), d, turn)
            e_s[i * span:(i + 1) * span, :size] = e
            d_s[i * span:(i + 1) * span, :size] = d
            tops.append(state[0])
        top, norm, delta = state
        delta = delta / norm
        live = token < length
        total_ref[0:1, start:stop] = jnp.where(live, top + jnp.log2(norm), -FILL)
        total_ref[1:2, start:stop] = delta
        inverse = jnp.where(live, 1.0 / norm, 0.0)
        for i in range(chunks):
            lo, hi = i * span, (i + 1) * span
            p = e_s[lo:hi, :size] * (jnp.exp2(tops[i] - top) * inverse)
            pb = p.astype(bf16)
            sb = (p * (d_s[lo:hi, :size] - delta)).astype(bf16)
            pb_s[lo:hi, :size] = pb
            sb_s[lo:hi, :size] = sb
            dv, dk = dot(pb, g), dot(sb, q)
            if start == 0:
                dv_s[lo:hi, :] = dv
                dk_s[lo:hi, :] = dk
            else:
                dv_s[lo:hi, :] += dv
                dk_s[lo:hi, :] += dk
        ot_ref[:, start:stop] = dot(values_t[...], pb_s[:, :size])
        qt_ref[:, start:stop] = dot(keys_t[...], sb_s[:, :size])
    for i in range(chunks):
        dk_refs[i][...] = (dk_s[i * span:(i + 1) * span, :] * scale).astype(bf16)
        dv_refs[i][...] = dv_s[i * span:(i + 1) * span, :].astype(bf16)


def near_kernel(group, chunks, scale, len_ref, x_ref, total_ref, ot_ref, qt_ref, *refs):
    kv_refs = refs[:chunks]
    out_ref = refs[chunks]
    grad_refs = refs[chunks + 1:2 * chunks + 1]
    q_s, g_s, keys_t, values_t, pb_s, sb_s, ot_s, qt_s, dk_s, dv_s = refs[2 * chunks + 1:]
    cap = x_ref.shape[0]
    span, head_dim = kv_refs[0].shape[1:]
    width = group * head_dim
    prefix = chunks * span
    length = len_ref[lax.axis_index("seq")]
    turn = scale * math.log2(math.e)
    stack_rows(x_ref, q_s, g_s, group)

    def pair(i):
        if i < chunks:
            return kv_refs[i][0], kv_refs[i][1]
        return x_ref[:, 2 * width:2 * width + head_dim], x_ref[:, 2 * width + head_dim:]

    bounds = [(i * span, (i + 1) * span) for i in range(chunks)] + [(prefix, prefix + cap)]
    for i, (lo, hi) in enumerate(bounds):
        k, v = pair(i)
        keys_t[:, lo:hi] = transposed(k)
        values_t[:, lo:hi] = transposed(v)
    for start, stop, token in blocks_of(group * cap, cap):
        size = stop - start
        q, g = q_s[start:stop, :], g_s[start:stop, :]
        total = total_ref[0:1, start:stop]
        delta = total_ref[1:2, start:stop]
        for i, (lo, hi) in enumerate(bounds):
            k, v = pair(i)
            p = jnp.exp2(dot_t(k, q) * turn - total)
            if i == chunks:
                p = jnp.where(causal(token, length, cap), p, 0.0)
            pb = p.astype(bf16)
            sb = (p * (dot_t(v, g) - delta)).astype(bf16)
            pb_s[lo:hi, :size] = pb
            sb_s[lo:hi, :size] = sb
            dv, dk = dot(pb, g), dot(sb, q)
            if start == 0:
                dv_s[lo:hi, :] = dv
                dk_s[lo:hi, :] = dk
            else:
                dv_s[lo:hi, :] += dv
                dk_s[lo:hi, :] += dk
        ot_s[:, start:stop] = ot_ref[:, start:stop] + dot(values_t[...], pb_s[:, :size])
        qt_s[:, start:stop] = qt_ref[:, start:stop] + dot(keys_t[...], sb_s[:, :size])
    for i in range(chunks):
        lo, hi = bounds[i]
        grad_refs[i][0] = dk_s[lo:hi, :] * scale
        grad_refs[i][1] = dv_s[lo:hi, :]
    out_ref[:, 2 * width:2 * width + head_dim] = (dk_s[prefix:, :] * scale).astype(bf16)
    out_ref[:, 2 * width + head_dim:] = dv_s[prefix:, :].astype(bf16)
    out = ot_s[...].T
    grad_q = (qt_s[...] * scale).T
    for i in range(group):
        out_ref[:, i * head_dim:(i + 1) * head_dim] = out[i * cap:(i + 1) * cap].astype(bf16)
        out_ref[:, width + i * head_dim:width + (i + 1) * head_dim] = (
            grad_q[i * cap:(i + 1) * cap].astype(bf16)
        )


def call(body, micros, ins, outs, scratch, limit):
    smem = pl.BlockSpec(memory_space=pltpu.SMEM)
    vmem = pl.BlockSpec(memory_space=pltpu.VMEM)
    return pl.pallas_call(
        body,
        out_shape=outs,
        in_specs=[smem] + [vmem] * (len(ins) - 1),
        out_specs=[vmem] * len(outs),
        scratch_shapes=scratch,
        compiler_params=pltpu.CompilerParams(vmem_limit_bytes=limit * 1024 * 1024),
        cost_estimate=pl.CostEstimate(
            flops=int(micros * 1.15e9),
            bytes_accessed=sum(x.size * x.dtype.itemsize for x in ins + outs),
            transcendentals=0,
        ),
    )(*ins)


def near_stats(lengths, x, shards, group, scale):
    cap = x.shape[0]
    _, span, head_dim = shards[0].shape
    rows = group * cap
    return call(
        functools.partial(near_stats_kernel, group, len(shards), scale),
        1.5,
        [lengths, x, *shards],
        [jax.ShapeDtypeStruct((3, rows), f32)],
        [VMEM((rows, head_dim), bf16)] * 2,
        12,
    )[0]


def far_pass(lengths, x, stats, shards, group, scale):
    cap = x.shape[0]
    _, span, head_dim = shards[0].shape
    chunks = len(shards)
    rows, keys = group * cap, chunks * span
    outs = call(
        functools.partial(far_kernel, group, chunks, scale),
        7.6,
        [lengths, x, stats, *shards],
        [jax.ShapeDtypeStruct(shard.shape, bf16) for shard in shards]
        + [jax.ShapeDtypeStruct((2, rows), f32)]
        + [jax.ShapeDtypeStruct((head_dim, rows), f32)] * 2,
        [VMEM((rows, head_dim), bf16)] * 2
        + [VMEM((head_dim, keys), bf16)] * 2
        + [VMEM((keys, 256), f32)] * 2
        + [VMEM((keys, 256), bf16)] * 2
        + [VMEM((keys, head_dim), f32)] * 2,
        24,
    )
    return outs[:chunks], outs[chunks:]


def near_pass(lengths, x, totals, shards, group, scale):
    cap, packed = x.shape
    _, span, head_dim = shards[0].shape
    rows, keys = group * cap, len(shards) * span + cap
    outs = call(
        functools.partial(near_kernel, group, len(shards), scale),
        4,
        [lengths, x, *totals, *shards],
        [jax.ShapeDtypeStruct((cap, packed), bf16)]
        + [jax.ShapeDtypeStruct(shard.shape, f32) for shard in shards],
        [VMEM((rows, head_dim), bf16)] * 2
        + [VMEM((head_dim, keys), bf16)] * 2
        + [VMEM((keys, 256), bf16)] * 2
        + [VMEM((head_dim, rows), f32)] * 2
        + [VMEM((keys, head_dim), f32)] * 2,
        24,
    )
    return outs[0], outs[1:]


def on_device(comp_q, comp_k, comp_v, comp_grad, prefix_k, prefix_v, comp_len):
    _, slots, heads, width = comp_q.shape
    head_dim = comp_k.shape[3]
    group = width // head_dim
    devices = lax.axis_size("seq")
    ring = devices // PROMPTS
    scale = 1.0 / math.sqrt(head_dim)

    to_prompt = []
    for owner in range(devices):
        plane, lane = divmod(owner, PROMPTS)
        reach = (0, 3, 1, 2)[lane]
        target = (plane + reach if plane % 2 else plane - reach) % ring
        to_prompt.append((owner, target * PROMPTS + owner // ring))
    to_owner = [(b, a) for a, b in to_prompt]

    def shift(x, steps):
        pairs = [(s, (s + PROMPTS * steps) % devices) for s in range(devices)]
        return lax.ppermute(x, "seq", pairs)

    own = lax.ppermute(jnp.stack([prefix_k[:, 0], prefix_v[:, 0]]), "seq", to_prompt)
    packed = pack(comp_q, comp_grad, comp_k, comp_v)
    own, packed = lax.optimization_barrier((own, packed))
    x = lax.all_to_all(packed, "head", split_axis=0, concat_axis=0, tiled=True)

    up, down = [own], [own]
    for step in range(1, ring // 2 + 1):
        up.append(shift(up[-1], 1))
        if step < ring - step:
            down.append(shift(down[-1], -1))

    far, steps = [], []
    for step in range(1, ring // 2 + 1):
        far.append(up[step])
        steps.append(-step)
        if step < ring - step:
            far.append(down[step])
            steps.append(step)
    stats = near_stats(comp_len, x, [own], group, scale)
    grads, totals = far_pass(comp_len, x, stats, far, group, scale)
    moved = [shift(grad, step) for grad, step in zip(grads, steps)]
    out, (own_grad,) = near_pass(comp_len, x, totals, [own], group, scale)
    own_grad, moved = lax.optimization_barrier((own_grad, moved))
    summed = own_grad
    for part in moved:
        summed = summed + part.astype(f32)
    back = lax.all_to_all(out, "head", split_axis=0, concat_axis=0, tiled=True)
    attn_out, grad_q, grad_k, grad_v = unpack(back, heads, width, head_dim)
    placed = lax.ppermute(summed.astype(bf16), "seq", to_owner).astype(f32)
    return (attn_out, grad_q, grad_k, grad_v, placed[0][:, None], placed[1][:, None])


def solution(mesh):
    tokens = P("seq", "head", None, None)
    prefix = P("seq", "head", None)
    return jax.shard_map(
        on_device,
        mesh=mesh,
        in_specs=(tokens, tokens, tokens, tokens, prefix, prefix, P()),
        out_specs=(tokens, tokens, tokens, tokens, prefix, prefix),
        check_vma=False,
    )
```

```python
import functools
import math

import jax
import jax.numpy as jnp
from jax import lax
from jax.experimental import pallas as pl
from jax.experimental.pallas import tpu as pltpu
from jax.sharding import PartitionSpec as P

PROMPTS = 4
FILL = -1e30
VMEM = pltpu.VMEM
LIMIT = 8 * 1024 * 1024
f32 = jnp.float32
bf16 = jnp.bfloat16


def dot(a, b):
    return jnp.dot(a, b, preferred_element_type=f32)


def dot_t(a, b):
    return lax.dot_general(a, b, (((1,), (1,)), ((), ())), preferred_element_type=f32)


def pack_kernel(heads, q_ref, g_ref, k_ref, v_ref, out_ref, wide):
    rows, width = q_ref.shape
    slots = rows // heads
    head_dim = k_ref.shape[1]
    group = width // head_dim
    for i in range(group):
        wide[i] = q_ref[:, i * head_dim:(i + 1) * head_dim].astype(f32)
        wide[group + i] = g_ref[:, i * head_dim:(i + 1) * head_dim].astype(f32)
    wide[2 * group] = k_ref[...].astype(f32)
    wide[2 * group + 1] = v_ref[...].astype(f32)
    for i in range(2 * group + 2):
        parts = [wide[i, pl.ds(h, slots, stride=heads), :] for h in range(heads)]
        out_ref[:, i * head_dim:(i + 1) * head_dim] = jnp.concatenate(parts, 0).astype(bf16)


def pack(q, g, k, v):
    _, slots, heads, width = q.shape
    head_dim = k.shape[3]
    rows = slots * heads
    total = 2 * width + 2 * head_dim
    return pl.pallas_call(
        functools.partial(pack_kernel, heads),
        out_shape=jax.ShapeDtypeStruct((rows, total), bf16),
        scratch_shapes=[VMEM((total // head_dim, rows, head_dim), f32)],
        compiler_params=pltpu.CompilerParams(vmem_limit_bytes=7 * LIMIT),
        cost_estimate=pl.CostEstimate(
            flops=int(2e9), bytes_accessed=4 * rows * total, transcendentals=0
        ),
    )(
        q.reshape(rows, width),
        g.reshape(rows, width),
        k.reshape(rows, head_dim),
        v.reshape(rows, head_dim),
    )


def unpack_kernel(heads, x_ref, o_ref, dq_ref, dk_ref, dv_ref, wide):
    rows, total = x_ref.shape
    slots = rows // heads
    width, head_dim = o_ref.shape[1], dk_ref.shape[1]
    for col in range(0, total, head_dim):
        wide[col // head_dim] = x_ref[:, col:col + head_dim].astype(f32)
    for col in range(0, total, head_dim):
        parts = [
            wide[col // head_dim, pl.ds(t, heads, stride=slots), :] for t in range(slots)
        ]
        block = jnp.concatenate(parts, 0).astype(bf16)
        if col < width:
            o_ref[:, col:col + head_dim] = block
        elif col < 2 * width:
            dq_ref[:, col - width:col - width + head_dim] = block
        elif col == 2 * width:
            dk_ref[...] = block
        else:
            dv_ref[...] = block


def unpack(x, heads, width, head_dim):
    rows, total = x.shape
    slots = rows // heads
    outs = pl.pallas_call(
        functools.partial(unpack_kernel, heads),
        out_shape=[
            jax.ShapeDtypeStruct((rows, width), bf16),
            jax.ShapeDtypeStruct((rows, width), bf16),
            jax.ShapeDtypeStruct((rows, head_dim), bf16),
            jax.ShapeDtypeStruct((rows, head_dim), bf16),
        ],
        scratch_shapes=[VMEM((total // head_dim, rows, head_dim), f32)],
        compiler_params=pltpu.CompilerParams(vmem_limit_bytes=LIMIT),
        cost_estimate=pl.CostEstimate(
            flops=int(1e9), bytes_accessed=4 * rows * total, transcendentals=0
        ),
    )(x)
    return [piece.reshape(1, slots, heads, piece.shape[1]) for piece in outs]


def stack_rows(x_ref, q_s, g_s, group):
    cap, head_dim = x_ref.shape[0], q_s.shape[1]
    width = group * head_dim
    for i in range(group):
        q_s[i * cap:(i + 1) * cap, :] = x_ref[:, i * head_dim:(i + 1) * head_dim]
        g_s[i * cap:(i + 1) * cap, :] = x_ref[:, width + i * head_dim:width + (i + 1) * head_dim]


def blocks_of(rows, cap):
    for start in range(0, rows, 256):
        stop = min(start + 256, rows)
        token = (lax.broadcasted_iota(jnp.int32, (1, stop - start), 1) + start) % cap
        yield start, stop, token


def causal(token, length, cap):
    key = lax.broadcasted_iota(jnp.int32, (cap, token.shape[1]), 0)
    return (key <= token) & (key < length)


def merge(state, s, d, turn, seen=None):
    if seen is not None:
        s = jnp.where(seen, s, FILL)
    high = jnp.max(s, axis=0, keepdims=True) * turn
    new = high if state is None else jnp.maximum(state[0], high)
    e = jnp.exp2(s * turn - new)
    if seen is not None:
        e = jnp.where(seen, e, 0.0)
    norm = jnp.sum(e, axis=0, keepdims=True)
    delta = jnp.sum(e * d, axis=0, keepdims=True)
    if state is not None:
        drop = jnp.exp2(state[0] - new)
        norm = norm + state[1] * drop
        delta = delta + state[2] * drop
    return e, (new, norm, delta)


def transposed(x):
    return x.astype(f32).T.astype(bf16)


def near_stats_kernel(group, chunks, scale, len_ref, x_ref, *refs):
    kv_refs, stats_ref, q_s, g_s = refs[:chunks], refs[chunks], refs[chunks + 1], refs[chunks + 2]
    cap, head_dim = x_ref.shape[0], q_s.shape[1]
    width = group * head_dim
    length = len_ref[lax.axis_index("seq")]
    turn = scale * math.log2(math.e)
    stack_rows(x_ref, q_s, g_s, group)
    for start, stop, token in blocks_of(group * cap, cap):
        q, g = q_s[start:stop, :], g_s[start:stop, :]
        state = None
        for kv in kv_refs:
            _, state = merge(state, dot_t(kv[0], q), dot_t(kv[1], g), turn)
        own_k = x_ref[:, 2 * width:2 * width + head_dim]
        own_v = x_ref[:, 2 * width + head_dim:]
        seen = causal(token, length, cap)
        _, state = merge(state, dot_t(own_k, q), dot_t(own_v, g), turn, seen)
        for i in range(3):
            stats_ref[i:i + 1, start:stop] = state[i]


def far_kernel(group, chunks, scale, len_ref, x_ref, stats_ref, *refs):
    shard_refs, grad_refs = refs[:chunks], refs[chunks:2 * chunks]
    k_refs, v_refs = [[r.at[i] for r in shard_refs] for i in range(2)]
    dk_refs, dv_refs = [[r.at[i] for r in grad_refs] for i in range(2)]
    (total_ref, ot_ref, qt_ref,
     q_s, g_s, keys_t, values_t, e_s, d_s, pb_s, sb_s, dk_s, dv_s) = refs[2 * chunks:]
    cap = x_ref.shape[0]
    span, head_dim = shard_refs[0].shape[1:]
    length = len_ref[lax.axis_index("seq")]
    turn = scale * math.log2(math.e)
    stack_rows(x_ref, q_s, g_s, group)
    for i in range(chunks):
        keys_t[:, i * span:(i + 1) * span] = transposed(k_refs[i][...])
        values_t[:, i * span:(i + 1) * span] = transposed(v_refs[i][...])
    for start, stop, token in blocks_of(group * cap, cap):
        size = stop - start
        q, g = q_s[start:stop, :], g_s[start:stop, :]
        state = tuple(stats_ref[i:i + 1, start:stop] for i in range(3))
        tops = []
        for i in range(chunks):
            d = dot_t(v_refs[i][...], g)
            e, state = merge(state, dot_t(k_refs[i][...], q), d, turn)
            e_s[i * span:(i + 1) * span, :size] = e
            d_s[i * span:(i + 1) * span, :size] = d
            tops.append(state[0])
        top, norm, delta = state
        delta = delta / norm
        live = token < length
        total_ref[0:1, start:stop] = jnp.where(live, top + jnp.log2(norm), -FILL)
        total_ref[1:2, start:stop] = delta
        inverse = jnp.where(live, 1.0 / norm, 0.0)
        for i in range(chunks):
            lo, hi = i * span, (i + 1) * span
            p = e_s[lo:hi, :size] * (jnp.exp2(tops[i] - top) * inverse)
            pb = p.astype(bf16)
            sb = (p * (d_s[lo:hi, :size] - delta)).astype(bf16)
            pb_s[lo:hi, :size] = pb
            sb_s[lo:hi, :size] = sb
            dv, dk = dot(pb, g), dot(sb, q)
            if start == 0:
                dv_s[lo:hi, :] = dv
                dk_s[lo:hi, :] = dk
            else:
                dv_s[lo:hi, :] += dv
                dk_s[lo:hi, :] += dk
        ot_ref[:, start:stop] = dot(values_t[...], pb_s[:, :size])
        qt_ref[:, start:stop] = dot(keys_t[...], sb_s[:, :size])
    for i in range(chunks):
        dk_refs[i][...] = (dk_s[i * span:(i + 1) * span, :] * scale).astype(bf16)
        dv_refs[i][...] = dv_s[i * span:(i + 1) * span, :].astype(bf16)


def near_kernel(group, chunks, scale, len_ref, x_ref, total_ref, ot_ref, qt_ref, *refs):
    kv_refs = refs[:chunks]
    out_ref = refs[chunks]
    grad_refs = refs[chunks + 1:2 * chunks + 1]
    q_s, g_s, keys_t, values_t, pb_s, sb_s, ot_s, qt_s, dk_s, dv_s = refs[2 * chunks + 1:]
    cap = x_ref.shape[0]
    span, head_dim = kv_refs[0].shape[1:]
    width = group * head_dim
    prefix = chunks * span
    length = len_ref[lax.axis_index("seq")]
    turn = scale * math.log2(math.e)
    stack_rows(x_ref, q_s, g_s, group)

    def pair(i):
        if i < chunks:
            return kv_refs[i][0], kv_refs[i][1]
        return x_ref[:, 2 * width:2 * width + head_dim], x_ref[:, 2 * width + head_dim:]

    bounds = [(i * span, (i + 1) * span) for i in range(chunks)] + [(prefix, prefix + cap)]
    for i, (lo, hi) in enumerate(bounds):
        k, v = pair(i)
        keys_t[:, lo:hi] = transposed(k)
        values_t[:, lo:hi] = transposed(v)
    for start, stop, token in blocks_of(group * cap, cap):
        size = stop - start
        q, g = q_s[start:stop, :], g_s[start:stop, :]
        total = total_ref[0:1, start:stop]
        delta = total_ref[1:2, start:stop]
        for i, (lo, hi) in enumerate(bounds):
            k, v = pair(i)
            p = jnp.exp2(dot_t(k, q) * turn - total)
            if i == chunks:
                p = jnp.where(causal(token, length, cap), p, 0.0)
            pb = p.astype(bf16)
            sb = (p * (dot_t(v, g) - delta)).astype(bf16)
            pb_s[lo:hi, :size] = pb
            sb_s[lo:hi, :size] = sb
            dv, dk = dot(pb, g), dot(sb, q)
            if start == 0:
                dv_s[lo:hi, :] = dv
                dk_s[lo:hi, :] = dk
            else:
                dv_s[lo:hi, :] += dv
                dk_s[lo:hi, :] += dk
        ot_s[:, start:stop] = ot_ref[:, start:stop] + dot(values_t[...], pb_s[:, :size])
        qt_s[:, start:stop] = qt_ref[:, start:stop] + dot(keys_t[...], sb_s[:, :size])
    for i in range(chunks):
        lo, hi = bounds[i]
        grad_refs[i][0] = dk_s[lo:hi, :] * scale
        grad_refs[i][1] = dv_s[lo:hi, :]
    out_ref[:, 2 * width:2 * width + head_dim] = (dk_s[prefix:, :] * scale).astype(bf16)
    out_ref[:, 2 * width + head_dim:] = dv_s[prefix:, :].astype(bf16)
    out = ot_s[...].T
    grad_q = (qt_s[...] * scale).T
    for i in range(group):
        out_ref[:, i * head_dim:(i + 1) * head_dim] = out[i * cap:(i + 1) * cap].astype(bf16)
        out_ref[:, width + i * head_dim:width + (i + 1) * head_dim] = (
            grad_q[i * cap:(i + 1) * cap].astype(bf16)
        )


def call(body, micros, ins, outs, scratch, limit, scalars=1):
    smem = pl.BlockSpec(memory_space=pltpu.SMEM)
    vmem = pl.BlockSpec(memory_space=pltpu.VMEM)
    return pl.pallas_call(
        body,
        out_shape=outs,
        in_specs=[smem] * scalars + [vmem] * (len(ins) - scalars),
        out_specs=[vmem] * len(outs),
        scratch_shapes=scratch,
        compiler_params=pltpu.CompilerParams(vmem_limit_bytes=limit * 1024 * 1024),
        cost_estimate=pl.CostEstimate(
            flops=int(micros * 1.15e9),
            bytes_accessed=sum(x.size * x.dtype.itemsize for x in ins + outs),
            transcendentals=0,
        ),
    )(*ins)


def near_stats(lengths, x, shards, group, scale):
    cap = x.shape[0]
    _, span, head_dim = shards[0].shape
    rows = group * cap
    return call(
        functools.partial(near_stats_kernel, group, len(shards), scale),
        1.5,
        [lengths, x, *shards],
        [jax.ShapeDtypeStruct((3, rows), f32)],
        [VMEM((rows, head_dim), bf16)] * 2,
        12,
    )[0]


def far_pass(lengths, x, stats, shards, group, scale):
    cap = x.shape[0]
    _, span, head_dim = shards[0].shape
    chunks = len(shards)
    rows, keys = group * cap, chunks * span
    outs = call(
        functools.partial(far_kernel, group, chunks, scale),
        7.6,
        [lengths, x, stats, *shards],
        [jax.ShapeDtypeStruct(shard.shape, bf16) for shard in shards]
        + [jax.ShapeDtypeStruct((2, rows), f32)]
        + [jax.ShapeDtypeStruct((head_dim, rows), f32)] * 2,
        [VMEM((rows, head_dim), bf16)] * 2
        + [VMEM((head_dim, keys), bf16)] * 2
        + [VMEM((keys, 256), f32)] * 2
        + [VMEM((keys, 256), bf16)] * 2
        + [VMEM((keys, head_dim), f32)] * 2,
        24,
    )
    return outs[:chunks], outs[chunks:]


def near_pass(lengths, x, totals, shards, group, scale):
    cap, packed = x.shape
    _, span, head_dim = shards[0].shape
    rows, keys = group * cap, len(shards) * span + cap
    outs = call(
        functools.partial(near_kernel, group, len(shards), scale),
        4,
        [lengths, x, *totals, *shards],
        [jax.ShapeDtypeStruct((cap, packed), bf16)]
        + [jax.ShapeDtypeStruct(shard.shape, f32) for shard in shards],
        [VMEM((rows, head_dim), bf16)] * 2
        + [VMEM((head_dim, keys), bf16)] * 2
        + [VMEM((keys, 256), bf16)] * 2
        + [VMEM((head_dim, rows), f32)] * 2
        + [VMEM((keys, head_dim), f32)] * 2,
        24,
    )
    return outs[0], outs[1:]


def sum_kernel(own_ref, *refs):
    total = own_ref[...]
    for ref in refs[:-1]:
        total = total + ref[...].astype(f32)
    refs[-1][...] = total.astype(bf16)


def add_parts(own, parts):
    return call(
        sum_kernel, 12, [own, *parts], [jax.ShapeDtypeStruct(own.shape, bf16)], [], 8, scalars=0
    )[0]


def on_device(comp_q, comp_k, comp_v, comp_grad, prefix_k, prefix_v, comp_len):
    _, slots, heads, width = comp_q.shape
    head_dim = comp_k.shape[3]
    group = width // head_dim
    devices = lax.axis_size("seq")
    ring = devices // PROMPTS
    scale = 1.0 / math.sqrt(head_dim)

    to_prompt = []
    for owner in range(devices):
        plane, lane = divmod(owner, PROMPTS)
        reach = (0, 3, 1, 2)[lane]
        target = (plane + reach if plane % 2 else plane - reach) % ring
        to_prompt.append((owner, target * PROMPTS + owner // ring))
    to_owner = [(b, a) for a, b in to_prompt]

    def shift(x, steps):
        way = (PROMPTS * steps, -PROMPTS * steps)
        pairs = [(s, (s + way[s % 2]) % devices) for s in range(devices)]
        return lax.ppermute(x, "seq", pairs)

    own = lax.ppermute(jnp.stack([prefix_k[:, 0], prefix_v[:, 0]]), "seq", to_prompt)
    packed = pack(comp_q, comp_grad, comp_k, comp_v)
    own, _ = lax.optimization_barrier((own, packed))
    x = lax.all_to_all(packed, "head", split_axis=0, concat_axis=0, tiled=True)

    up, down = [own], [own]
    for step in range(1, ring // 2 + 1):
        up.append(shift(up[-1], 1))
        if step < ring - step:
            down.append(shift(down[-1], -1))

    far, steps = [], []
    for step in range(1, ring // 2 + 1):
        far.append(up[step])
        steps.append(-step)
        if step < ring - step:
            far.append(down[step])
            steps.append(step)
    stats = near_stats(comp_len, x, [own], group, scale)
    grads, totals = far_pass(comp_len, x, stats, far, group, scale)
    moved = [shift(grad, step) for grad, step in zip(grads, steps)]
    out, (own_grad,) = near_pass(comp_len, x, totals, [own], group, scale)
    summed = add_parts(own_grad, moved)
    back = lax.all_to_all(out, "head", split_axis=0, concat_axis=0, tiled=True)
    attn_out, grad_q, grad_k, grad_v = unpack(back, heads, width, head_dim)
    placed = lax.ppermute(summed, "seq", to_owner)
    placed, (attn_out, grad_q, grad_k, grad_v) = lax.optimization_barrier(
        (placed, (attn_out, grad_q, grad_k, grad_v))
    )
    placed = placed.astype(f32)
    return (attn_out, grad_q, grad_k, grad_v, placed[0][:, None], placed[1][:, None])


def solution(mesh):
    tokens = P("seq", "head", None, None)
    prefix = P("seq", "head", None)
    return jax.shard_map(
        on_device,
        mesh=mesh,
        in_specs=(tokens, tokens, tokens, tokens, prefix, prefix, P()),
        out_specs=(tokens, tokens, tokens, tokens, prefix, prefix),
        check_vma=False,
    )
```

```python
import functools
import math

import jax
import jax.numpy as jnp
from jax import lax
from jax.experimental import pallas as pl
from jax.experimental.pallas import tpu as pltpu
from jax.sharding import PartitionSpec as P

PROMPTS = 4
FILL = -1e30
VMEM = pltpu.VMEM
LIMIT = 8 * 1024 * 1024
f32 = jnp.float32
bf16 = jnp.bfloat16


def dot(a, b):
    return jnp.dot(a, b, preferred_element_type=f32)


def dot_t(a, b):
    return lax.dot_general(a, b, (((1,), (1,)), ((), ())), preferred_element_type=f32)


def pack_kernel(heads, q_ref, g_ref, k_ref, v_ref, out_ref, wide):
    rows, width = q_ref.shape
    slots = rows // heads
    head_dim = k_ref.shape[1]
    group = width // head_dim
    for i in range(group):
        wide[i] = q_ref[:, i * head_dim:(i + 1) * head_dim].astype(f32)
        wide[group + i] = g_ref[:, i * head_dim:(i + 1) * head_dim].astype(f32)
    wide[2 * group] = k_ref[...].astype(f32)
    wide[2 * group + 1] = v_ref[...].astype(f32)
    for i in range(2 * group + 2):
        parts = [wide[i, pl.ds(h, slots, stride=heads), :] for h in range(heads)]
        out_ref[:, i * head_dim:(i + 1) * head_dim] = jnp.concatenate(parts, 0).astype(bf16)


def pack(q, g, k, v):
    _, slots, heads, width = q.shape
    head_dim = k.shape[3]
    rows = slots * heads
    total = 2 * width + 2 * head_dim
    return pl.pallas_call(
        functools.partial(pack_kernel, heads),
        out_shape=jax.ShapeDtypeStruct((rows, total), bf16),
        scratch_shapes=[VMEM((total // head_dim, rows, head_dim), f32)],
        compiler_params=pltpu.CompilerParams(vmem_limit_bytes=7 * LIMIT),
        cost_estimate=pl.CostEstimate(
            flops=int(2e9), bytes_accessed=4 * rows * total, transcendentals=0
        ),
    )(
        q.reshape(rows, width),
        g.reshape(rows, width),
        k.reshape(rows, head_dim),
        v.reshape(rows, head_dim),
    )


def unpack_kernel(heads, x_ref, o_ref, dq_ref, dk_ref, dv_ref, wide):
    rows, total = x_ref.shape
    slots = rows // heads
    width, head_dim = o_ref.shape[1], dk_ref.shape[1]
    for col in range(0, total, head_dim):
        wide[col // head_dim] = x_ref[:, col:col + head_dim].astype(f32)
    for col in range(0, total, head_dim):
        parts = [
            wide[col // head_dim, pl.ds(t, heads, stride=slots), :] for t in range(slots)
        ]
        block = jnp.concatenate(parts, 0).astype(bf16)
        if col < width:
            o_ref[:, col:col + head_dim] = block
        elif col < 2 * width:
            dq_ref[:, col - width:col - width + head_dim] = block
        elif col == 2 * width:
            dk_ref[...] = block
        else:
            dv_ref[...] = block


def unpack(x, heads, width, head_dim):
    rows, total = x.shape
    slots = rows // heads
    outs = pl.pallas_call(
        functools.partial(unpack_kernel, heads),
        out_shape=[
            jax.ShapeDtypeStruct((rows, width), bf16),
            jax.ShapeDtypeStruct((rows, width), bf16),
            jax.ShapeDtypeStruct((rows, head_dim), bf16),
            jax.ShapeDtypeStruct((rows, head_dim), bf16),
        ],
        scratch_shapes=[VMEM((total // head_dim, rows, head_dim), f32)],
        compiler_params=pltpu.CompilerParams(vmem_limit_bytes=LIMIT),
        cost_estimate=pl.CostEstimate(
            flops=int(1e9), bytes_accessed=4 * rows * total, transcendentals=0
        ),
    )(x)
    return [piece.reshape(1, slots, heads, piece.shape[1]) for piece in outs]


def stack_rows(x_ref, q_s, g_s, group):
    cap, head_dim = x_ref.shape[0], q_s.shape[1]
    width = group * head_dim
    for i in range(group):
        q_s[i * cap:(i + 1) * cap, :] = x_ref[:, i * head_dim:(i + 1) * head_dim]
        g_s[i * cap:(i + 1) * cap, :] = x_ref[:, width + i * head_dim:width + (i + 1) * head_dim]


def blocks_of(rows, cap):
    for start in range(0, rows, 256):
        stop = min(start + 256, rows)
        token = (lax.broadcasted_iota(jnp.int32, (1, stop - start), 1) + start) % cap
        yield start, stop, token


def causal(token, length, cap):
    key = lax.broadcasted_iota(jnp.int32, (cap, token.shape[1]), 0)
    return (key <= token) & (key < length)


def merge(state, s, d, turn, seen=None):
    if seen is not None:
        s = jnp.where(seen, s, FILL)
    high = jnp.max(s, axis=0, keepdims=True) * turn
    new = high if state is None else jnp.maximum(state[0], high)
    e = jnp.exp2(s * turn - new)
    if seen is not None:
        e = jnp.where(seen, e, 0.0)
    norm = jnp.sum(e, axis=0, keepdims=True)
    delta = jnp.sum(e * d, axis=0, keepdims=True)
    if state is not None:
        drop = jnp.exp2(state[0] - new)
        norm = norm + state[1] * drop
        delta = delta + state[2] * drop
    return e, (new, norm, delta)


def transposed(x):
    return x.astype(f32).T.astype(bf16)


def near_stats_kernel(group, chunks, scale, len_ref, x_ref, *refs):
    kv_refs, stats_ref, q_s, g_s = refs[:chunks], refs[chunks], refs[chunks + 1], refs[chunks + 2]
    cap, head_dim = x_ref.shape[0], q_s.shape[1]
    width = group * head_dim
    length = len_ref[lax.axis_index("seq")]
    turn = scale * math.log2(math.e)
    stack_rows(x_ref, q_s, g_s, group)
    for start, stop, token in blocks_of(group * cap, cap):
        q, g = q_s[start:stop, :], g_s[start:stop, :]
        state = None
        for kv in kv_refs:
            _, state = merge(state, dot_t(kv[0], q), dot_t(kv[1], g), turn)
        own_k = x_ref[:, 2 * width:2 * width + head_dim]
        own_v = x_ref[:, 2 * width + head_dim:]
        seen = causal(token, length, cap)
        _, state = merge(state, dot_t(own_k, q), dot_t(own_v, g), turn, seen)
        for i in range(3):
            stats_ref[i:i + 1, start:stop] = state[i]


def far_kernel(group, chunks, scale, len_ref, x_ref, stats_ref, *refs):
    pairs = chunks // 2
    shard_refs, grad_refs = refs[:pairs], refs[pairs:2 * pairs]
    k_refs, v_refs = [[r.at[j, i] for r in shard_refs for j in range(2)] for i in range(2)]
    dk_refs, dv_refs = [[r.at[j, i] for r in grad_refs for j in range(2)] for i in range(2)]
    (total_ref, ot_ref, qt_ref,
     q_s, g_s, keys_t, values_t, e_s, d_s, pb_s, sb_s, dk_s, dv_s) = refs[2 * pairs:]
    cap = x_ref.shape[0]
    span, head_dim = shard_refs[0].shape[2:]
    length = len_ref[lax.axis_index("seq")]
    turn = scale * math.log2(math.e)
    stack_rows(x_ref, q_s, g_s, group)
    for i in range(chunks):
        keys_t[:, i * span:(i + 1) * span] = transposed(k_refs[i][...])
        values_t[:, i * span:(i + 1) * span] = transposed(v_refs[i][...])
    for start, stop, token in blocks_of(group * cap, cap):
        size = stop - start
        q, g = q_s[start:stop, :], g_s[start:stop, :]
        state = tuple(stats_ref[i:i + 1, start:stop] for i in range(3))
        tops = []
        for i in range(chunks):
            d = dot_t(v_refs[i][...], g)
            e, state = merge(state, dot_t(k_refs[i][...], q), d, turn)
            e_s[i * span:(i + 1) * span, :size] = e
            d_s[i * span:(i + 1) * span, :size] = d
            tops.append(state[0])
        top, norm, delta = state
        delta = delta / norm
        live = token < length
        total_ref[0:1, start:stop] = jnp.where(live, top + jnp.log2(norm), -FILL)
        total_ref[1:2, start:stop] = delta
        inverse = jnp.where(live, 1.0 / norm, 0.0)
        for i in range(chunks):
            lo, hi = i * span, (i + 1) * span
            p = e_s[lo:hi, :size] * (jnp.exp2(tops[i] - top) * inverse)
            pb = p.astype(bf16)
            sb = (p * (d_s[lo:hi, :size] - delta)).astype(bf16)
            pb_s[lo:hi, :size] = pb
            sb_s[lo:hi, :size] = sb
            dv, dk = dot(pb, g), dot(sb, q)
            if start == 0:
                dv_s[lo:hi, :] = dv
                dk_s[lo:hi, :] = dk
            else:
                dv_s[lo:hi, :] += dv
                dk_s[lo:hi, :] += dk
        ot_ref[:, start:stop] = dot(values_t[...], pb_s[:, :size])
        qt_ref[:, start:stop] = dot(keys_t[...], sb_s[:, :size])
    for i in range(chunks):
        dk_refs[i][...] = (dk_s[i * span:(i + 1) * span, :] * scale).astype(bf16)
        dv_refs[i][...] = dv_s[i * span:(i + 1) * span, :].astype(bf16)


def near_kernel(group, chunks, scale, len_ref, x_ref, total_ref, ot_ref, qt_ref, *refs):
    kv_refs = refs[:chunks]
    out_ref = refs[chunks]
    grad_refs = refs[chunks + 1:2 * chunks + 1]
    q_s, g_s, keys_t, values_t, pb_s, sb_s, ot_s, qt_s, dk_s, dv_s = refs[2 * chunks + 1:]
    cap = x_ref.shape[0]
    span, head_dim = kv_refs[0].shape[1:]
    width = group * head_dim
    prefix = chunks * span
    length = len_ref[lax.axis_index("seq")]
    turn = scale * math.log2(math.e)
    stack_rows(x_ref, q_s, g_s, group)

    def pair(i):
        if i < chunks:
            return kv_refs[i][0], kv_refs[i][1]
        return x_ref[:, 2 * width:2 * width + head_dim], x_ref[:, 2 * width + head_dim:]

    bounds = [(i * span, (i + 1) * span) for i in range(chunks)] + [(prefix, prefix + cap)]
    for i, (lo, hi) in enumerate(bounds):
        k, v = pair(i)
        keys_t[:, lo:hi] = transposed(k)
        values_t[:, lo:hi] = transposed(v)
    for start, stop, token in blocks_of(group * cap, cap):
        size = stop - start
        q, g = q_s[start:stop, :], g_s[start:stop, :]
        total = total_ref[0:1, start:stop]
        delta = total_ref[1:2, start:stop]
        for i, (lo, hi) in enumerate(bounds):
            k, v = pair(i)
            p = jnp.exp2(dot_t(k, q) * turn - total)
            if i == chunks:
                p = jnp.where(causal(token, length, cap), p, 0.0)
            pb = p.astype(bf16)
            sb = (p * (dot_t(v, g) - delta)).astype(bf16)
            pb_s[lo:hi, :size] = pb
            sb_s[lo:hi, :size] = sb
            dv, dk = dot(pb, g), dot(sb, q)
            if start == 0:
                dv_s[lo:hi, :] = dv
                dk_s[lo:hi, :] = dk
            else:
                dv_s[lo:hi, :] += dv
                dk_s[lo:hi, :] += dk
        ot_s[:, start:stop] = ot_ref[:, start:stop] + dot(values_t[...], pb_s[:, :size])
        qt_s[:, start:stop] = qt_ref[:, start:stop] + dot(keys_t[...], sb_s[:, :size])
    for i in range(chunks):
        lo, hi = bounds[i]
        grad_refs[i][0] = dk_s[lo:hi, :] * scale
        grad_refs[i][1] = dv_s[lo:hi, :]
    out_ref[:, 2 * width:2 * width + head_dim] = (dk_s[prefix:, :] * scale).astype(bf16)
    out_ref[:, 2 * width + head_dim:] = dv_s[prefix:, :].astype(bf16)
    out = ot_s[...].T
    grad_q = (qt_s[...] * scale).T
    for i in range(group):
        out_ref[:, i * head_dim:(i + 1) * head_dim] = out[i * cap:(i + 1) * cap].astype(bf16)
        out_ref[:, width + i * head_dim:width + (i + 1) * head_dim] = (
            grad_q[i * cap:(i + 1) * cap].astype(bf16)
        )


def call(body, micros, ins, outs, scratch, limit, scalars=1):
    smem = pl.BlockSpec(memory_space=pltpu.SMEM)
    vmem = pl.BlockSpec(memory_space=pltpu.VMEM)
    return pl.pallas_call(
        body,
        out_shape=outs,
        in_specs=[smem] * scalars + [vmem] * (len(ins) - scalars),
        out_specs=[vmem] * len(outs),
        scratch_shapes=scratch,
        compiler_params=pltpu.CompilerParams(vmem_limit_bytes=limit * 1024 * 1024),
        cost_estimate=pl.CostEstimate(
            flops=int(micros * 1.15e9),
            bytes_accessed=sum(x.size * x.dtype.itemsize for x in ins + outs),
            transcendentals=0,
        ),
    )(*ins)


def near_stats(lengths, x, shards, group, scale):
    cap = x.shape[0]
    _, span, head_dim = shards[0].shape
    rows = group * cap
    return call(
        functools.partial(near_stats_kernel, group, len(shards), scale),
        2,
        [lengths, x, *shards],
        [jax.ShapeDtypeStruct((3, rows), f32)],
        [VMEM((rows, head_dim), bf16)] * 2,
        12,
    )[0]


def far_pass(lengths, x, stats, shards, group, scale):
    cap = x.shape[0]
    span, head_dim = shards[0].shape[2:]
    chunks = 2 * len(shards)
    rows, keys = group * cap, chunks * span
    outs = call(
        functools.partial(far_kernel, group, chunks, scale),
        6.5,
        [lengths, x, stats, *shards],
        [jax.ShapeDtypeStruct(shard.shape, bf16) for shard in shards]
        + [jax.ShapeDtypeStruct((2, rows), f32)]
        + [jax.ShapeDtypeStruct((head_dim, rows), f32)] * 2,
        [VMEM((rows, head_dim), bf16)] * 2
        + [VMEM((head_dim, keys), bf16)] * 2
        + [VMEM((keys, 256), f32)] * 2
        + [VMEM((keys, 256), bf16)] * 2
        + [VMEM((keys, head_dim), f32)] * 2,
        24,
    )
    return outs[:len(shards)], outs[len(shards):]


def near_pass(lengths, x, totals, shards, group, scale):
    cap, packed = x.shape
    _, span, head_dim = shards[0].shape
    rows, keys = group * cap, len(shards) * span + cap
    outs = call(
        functools.partial(near_kernel, group, len(shards), scale),
        5,
        [lengths, x, *totals, *shards],
        [jax.ShapeDtypeStruct((cap, packed), bf16)]
        + [jax.ShapeDtypeStruct(shard.shape, f32) for shard in shards],
        [VMEM((rows, head_dim), bf16)] * 2
        + [VMEM((head_dim, keys), bf16)] * 2
        + [VMEM((keys, 256), bf16)] * 2
        + [VMEM((head_dim, rows), f32)] * 2
        + [VMEM((keys, head_dim), f32)] * 2,
        24,
    )
    return outs[0], outs[1:]


def sum_kernel(count, *refs):
    for i in range(count):
        total = refs[i][...]
        for ref in refs[count:-count]:
            total = total + ref[i].astype(f32)
        refs[i - count][...] = total.astype(bf16)


def add_parts(held, parts):
    return call(
        functools.partial(sum_kernel, len(held)), 12, [*held, *parts],
        [jax.ShapeDtypeStruct(part.shape, bf16) for part in held], [], 8, scalars=0,
    )


def on_device(comp_q, comp_k, comp_v, comp_grad, prefix_k, prefix_v, comp_len):
    _, slots, heads, width = comp_q.shape
    head_dim = comp_k.shape[3]
    group = width // head_dim
    devices = lax.axis_size("seq")
    ring = devices // PROMPTS
    scale = 1.0 / math.sqrt(head_dim)

    holders = []
    for owner in range(devices):
        plane, lane = divmod(owner, PROMPTS)
        reach = (0, 3, 1, 2)[lane]
        holders.append((plane + reach if plane % 2 else plane - reach) % ring)

    def spread(steps):
        return [
            (owner, (holder + steps) % ring * PROMPTS + owner // ring)
            for owner, holder in enumerate(holders)
        ]

    def collect(x, steps):
        return lax.ppermute(x, "seq", [(b, a) for a, b in spread(steps)])

    def shift(x, steps):
        way = (PROMPTS * steps, -PROMPTS * steps)
        pairs = [(s, (s + way[s % 2]) % devices) for s in range(devices)]
        return lax.ppermute(x, "seq", pairs)

    half = ring // 2
    prefix = jnp.stack([prefix_k[:, 0], prefix_v[:, 0]])
    own, across = [lax.ppermute(prefix, "seq", spread(steps)) for steps in (0, half)]
    packed = pack(comp_q, comp_grad, comp_k, comp_v)
    own, across, _ = lax.optimization_barrier((own, across, packed))
    x = lax.all_to_all(packed, "head", split_axis=0, concat_axis=0, tiled=True)

    held, steps = [own, across], (1, -1, 2)
    both = jnp.stack(held)
    far = [shift(both, step) for step in steps]
    stats = near_stats(comp_len, x, held, group, scale)
    grads, totals = far_pass(comp_len, x, stats, far, group, scale)
    moved = [shift(grad, -step) for grad, step in zip(grads, steps)]
    out, held_grads = near_pass(comp_len, x, totals, held, group, scale)
    own, across = add_parts(held_grads, moved)
    back = lax.all_to_all(out, "head", split_axis=0, concat_axis=0, tiled=True)
    attn_out, grad_q, grad_k, grad_v = unpack(back, heads, width, head_dim)
    own, across = collect(own, 0), collect(across, half)
    own, across, (attn_out, grad_q, grad_k, grad_v) = lax.optimization_barrier(
        (own, across, (attn_out, grad_q, grad_k, grad_v))
    )
    placed = [own[i].astype(f32) + across[i].astype(f32) for i in range(2)]
    return (attn_out, grad_q, grad_k, grad_v, placed[0][:, None], placed[1][:, None])


def solution(mesh):
    tokens = P("seq", "head", None, None)
    prefix = P("seq", "head", None)
    return jax.shard_map(
        on_device,
        mesh=mesh,
        in_specs=(tokens, tokens, tokens, tokens, prefix, prefix, P()),
        out_specs=(tokens, tokens, tokens, tokens, prefix, prefix),
        check_vma=False,
    )
```

```python
import functools
import math

import jax
import jax.numpy as jnp
from jax import lax
from jax.experimental import pallas as pl
from jax.experimental.pallas import tpu as pltpu
from jax.sharding import PartitionSpec as P

PROMPTS = 4
FILL = -1e30
VMEM = pltpu.VMEM
LIMIT = 8 * 1024 * 1024
f32 = jnp.float32
bf16 = jnp.bfloat16


def dot(a, b):
    return jnp.dot(a, b, preferred_element_type=f32)


def dot_t(a, b):
    return lax.dot_general(a, b, (((1,), (1,)), ((), ())), preferred_element_type=f32)


def pack_kernel(heads, q_ref, g_ref, k_ref, v_ref, out_ref, wide):
    rows, width = q_ref.shape
    slots = rows // heads
    head_dim = k_ref.shape[1]
    group = width // head_dim
    for i in range(group):
        wide[i] = q_ref[:, i * head_dim:(i + 1) * head_dim].astype(f32)
        wide[group + i] = g_ref[:, i * head_dim:(i + 1) * head_dim].astype(f32)
    wide[2 * group] = k_ref[...].astype(f32)
    wide[2 * group + 1] = v_ref[...].astype(f32)
    for i in range(2 * group + 2):
        parts = [wide[i, pl.ds(h, slots, stride=heads), :] for h in range(heads)]
        out_ref[:, i * head_dim:(i + 1) * head_dim] = jnp.concatenate(parts, 0).astype(bf16)


def pack(q, g, k, v):
    _, slots, heads, width = q.shape
    head_dim = k.shape[3]
    rows = slots * heads
    total = 2 * width + 2 * head_dim
    return pl.pallas_call(
        functools.partial(pack_kernel, heads),
        out_shape=jax.ShapeDtypeStruct((rows, total), bf16),
        scratch_shapes=[VMEM((total // head_dim, rows, head_dim), f32)],
        compiler_params=pltpu.CompilerParams(vmem_limit_bytes=7 * LIMIT),
        cost_estimate=pl.CostEstimate(
            flops=int(2e9), bytes_accessed=4 * rows * total, transcendentals=0
        ),
    )(
        q.reshape(rows, width),
        g.reshape(rows, width),
        k.reshape(rows, head_dim),
        v.reshape(rows, head_dim),
    )


def unpack_kernel(heads, x_ref, o_ref, dq_ref, dk_ref, dv_ref, wide):
    rows, total = x_ref.shape
    slots = rows // heads
    width, head_dim = o_ref.shape[1], dk_ref.shape[1]
    for col in range(0, total, head_dim):
        wide[col // head_dim] = x_ref[:, col:col + head_dim].astype(f32)
    for col in range(0, total, head_dim):
        parts = [
            wide[col // head_dim, pl.ds(t, heads, stride=slots), :] for t in range(slots)
        ]
        block = jnp.concatenate(parts, 0).astype(bf16)
        if col < width:
            o_ref[:, col:col + head_dim] = block
        elif col < 2 * width:
            dq_ref[:, col - width:col - width + head_dim] = block
        elif col == 2 * width:
            dk_ref[...] = block
        else:
            dv_ref[...] = block


def unpack(x, heads, width, head_dim):
    rows, total = x.shape
    slots = rows // heads
    outs = pl.pallas_call(
        functools.partial(unpack_kernel, heads),
        out_shape=[
            jax.ShapeDtypeStruct((rows, width), bf16),
            jax.ShapeDtypeStruct((rows, width), bf16),
            jax.ShapeDtypeStruct((rows, head_dim), bf16),
            jax.ShapeDtypeStruct((rows, head_dim), bf16),
        ],
        scratch_shapes=[VMEM((total // head_dim, rows, head_dim), f32)],
        compiler_params=pltpu.CompilerParams(vmem_limit_bytes=LIMIT),
        cost_estimate=pl.CostEstimate(
            flops=int(1e9), bytes_accessed=4 * rows * total, transcendentals=0
        ),
    )(x)
    return [piece.reshape(1, slots, heads, piece.shape[1]) for piece in outs]


def stack_rows(x_ref, q_s, g_s, group):
    cap, head_dim = x_ref.shape[0], q_s.shape[1]
    width = group * head_dim
    for i in range(group):
        q_s[i * cap:(i + 1) * cap, :] = x_ref[:, i * head_dim:(i + 1) * head_dim]
        g_s[i * cap:(i + 1) * cap, :] = x_ref[:, width + i * head_dim:width + (i + 1) * head_dim]


def blocks_of(rows, cap):
    for start in range(0, rows, 256):
        stop = min(start + 256, rows)
        token = (lax.broadcasted_iota(jnp.int32, (1, stop - start), 1) + start) % cap
        yield start, stop, token


def causal(token, length, cap):
    key = lax.broadcasted_iota(jnp.int32, (cap, token.shape[1]), 0)
    return (key <= token) & (key < length)


def merge(state, s, d, turn, seen=None):
    if seen is not None:
        s = jnp.where(seen, s, FILL)
    high = jnp.max(s, axis=0, keepdims=True) * turn
    new = high if state is None else jnp.maximum(state[0], high)
    e = jnp.exp2(s * turn - new)
    if seen is not None:
        e = jnp.where(seen, e, 0.0)
    norm = jnp.sum(e, axis=0, keepdims=True)
    delta = jnp.sum(e * d, axis=0, keepdims=True)
    if state is not None:
        drop = jnp.exp2(state[0] - new)
        norm = norm + state[1] * drop
        delta = delta + state[2] * drop
    return e, (new, norm, delta)


def transposed(x):
    return x.astype(f32).T.astype(bf16)


def near_stats_kernel(group, chunks, scale, len_ref, x_ref, *refs):
    kv_refs, stats_ref, q_s, g_s = refs[:chunks], refs[chunks], refs[chunks + 1], refs[chunks + 2]
    cap, head_dim = x_ref.shape[0], q_s.shape[1]
    width = group * head_dim
    length = len_ref[lax.axis_index("seq")]
    turn = scale * math.log2(math.e)
    stack_rows(x_ref, q_s, g_s, group)
    for start, stop, token in blocks_of(group * cap, cap):
        q, g = q_s[start:stop, :], g_s[start:stop, :]
        state = None
        for kv in kv_refs:
            _, state = merge(state, dot_t(kv[0], q), dot_t(kv[1], g), turn)
        own_k = x_ref[:, 2 * width:2 * width + head_dim]
        own_v = x_ref[:, 2 * width + head_dim:]
        seen = causal(token, length, cap)
        _, state = merge(state, dot_t(own_k, q), dot_t(own_v, g), turn, seen)
        for i in range(3):
            stats_ref[i:i + 1, start:stop] = state[i]


def far_kernel(group, chunks, scale, len_ref, x_ref, stats_ref, *refs):
    pairs = chunks // 2
    shard_refs, grad_refs = refs[:pairs], refs[pairs:2 * pairs]
    k_refs, v_refs = [[r.at[j, i] for r in shard_refs for j in range(2)] for i in range(2)]
    dk_refs, dv_refs = [[r.at[j, i] for r in grad_refs for j in range(2)] for i in range(2)]
    (total_ref, ot_ref, qt_ref,
     q_s, g_s, keys_t, values_t, e_s, d_s, pb_s, sb_s, dk_s, dv_s) = refs[2 * pairs:]
    cap = x_ref.shape[0]
    span, head_dim = shard_refs[0].shape[2:]
    length = len_ref[lax.axis_index("seq")]
    turn = scale * math.log2(math.e)
    stack_rows(x_ref, q_s, g_s, group)
    for i in range(chunks):
        keys_t[:, i * span:(i + 1) * span] = transposed(k_refs[i][...])
        values_t[:, i * span:(i + 1) * span] = transposed(v_refs[i][...])
    for start, stop, token in blocks_of(group * cap, cap):
        size = stop - start
        q, g = q_s[start:stop, :], g_s[start:stop, :]
        state = tuple(stats_ref[i:i + 1, start:stop] for i in range(3))
        tops = []
        for i in range(chunks):
            d = dot_t(v_refs[i][...], g)
            e, state = merge(state, dot_t(k_refs[i][...], q), d, turn)
            e_s[i * span:(i + 1) * span, :size] = e
            d_s[i * span:(i + 1) * span, :size] = d
            tops.append(state[0])
        top, norm, delta = state
        delta = delta / norm
        live = token < length
        total_ref[0:1, start:stop] = jnp.where(live, top + jnp.log2(norm), -FILL)
        total_ref[1:2, start:stop] = delta
        inverse = jnp.where(live, 1.0 / norm, 0.0)
        for i in range(chunks):
            lo, hi = i * span, (i + 1) * span
            p = e_s[lo:hi, :size] * (jnp.exp2(tops[i] - top) * inverse)
            pb = p.astype(bf16)
            sb = (p * (d_s[lo:hi, :size] - delta)).astype(bf16)
            pb_s[lo:hi, :size] = pb
            sb_s[lo:hi, :size] = sb
            dv, dk = dot(pb, g), dot(sb, q)
            if start == 0:
                dv_s[lo:hi, :] = dv
                dk_s[lo:hi, :] = dk
            else:
                dv_s[lo:hi, :] += dv
                dk_s[lo:hi, :] += dk
        ot_ref[:, start:stop] = dot(values_t[...], pb_s[:, :size])
        qt_ref[:, start:stop] = dot(keys_t[...], sb_s[:, :size])
    for i in range(chunks):
        dk_refs[i][...] = (dk_s[i * span:(i + 1) * span, :] * scale).astype(bf16)
        dv_refs[i][...] = dv_s[i * span:(i + 1) * span, :].astype(bf16)


def near_kernel(group, chunks, scale, len_ref, x_ref, total_ref, ot_ref, qt_ref, *refs):
    kv_refs = refs[:chunks]
    out_ref = refs[chunks]
    grad_refs = refs[chunks + 1:2 * chunks + 1]
    q_s, g_s, keys_t, values_t, pb_s, sb_s, ot_s, qt_s, dk_s, dv_s = refs[2 * chunks + 1:]
    cap = x_ref.shape[0]
    span, head_dim = kv_refs[0].shape[1:]
    width = group * head_dim
    prefix = chunks * span
    length = len_ref[lax.axis_index("seq")]
    turn = scale * math.log2(math.e)
    stack_rows(x_ref, q_s, g_s, group)

    def pair(i):
        if i < chunks:
            return kv_refs[i][0], kv_refs[i][1]
        return x_ref[:, 2 * width:2 * width + head_dim], x_ref[:, 2 * width + head_dim:]

    bounds = [(i * span, (i + 1) * span) for i in range(chunks)] + [(prefix, prefix + cap)]
    for i, (lo, hi) in enumerate(bounds):
        k, v = pair(i)
        keys_t[:, lo:hi] = transposed(k)
        values_t[:, lo:hi] = transposed(v)
    for start, stop, token in blocks_of(group * cap, cap):
        size = stop - start
        q, g = q_s[start:stop, :], g_s[start:stop, :]
        total = total_ref[0:1, start:stop]
        delta = total_ref[1:2, start:stop]
        for i, (lo, hi) in enumerate(bounds):
            k, v = pair(i)
            p = jnp.exp2(dot_t(k, q) * turn - total)
            if i == chunks:
                p = jnp.where(causal(token, length, cap), p, 0.0)
            pb = p.astype(bf16)
            sb = (p * (dot_t(v, g) - delta)).astype(bf16)
            pb_s[lo:hi, :size] = pb
            sb_s[lo:hi, :size] = sb
            dv, dk = dot(pb, g), dot(sb, q)
            if start == 0:
                dv_s[lo:hi, :] = dv
                dk_s[lo:hi, :] = dk
            else:
                dv_s[lo:hi, :] += dv
                dk_s[lo:hi, :] += dk
        ot_s[:, start:stop] = ot_ref[:, start:stop] + dot(values_t[...], pb_s[:, :size])
        qt_s[:, start:stop] = qt_ref[:, start:stop] + dot(keys_t[...], sb_s[:, :size])
    for i in range(chunks):
        lo, hi = bounds[i]
        grad_refs[i][0] = dk_s[lo:hi, :] * scale
        grad_refs[i][1] = dv_s[lo:hi, :]
    out_ref[:, 2 * width:2 * width + head_dim] = (dk_s[prefix:, :] * scale).astype(bf16)
    out_ref[:, 2 * width + head_dim:] = dv_s[prefix:, :].astype(bf16)
    out = ot_s[...].T
    grad_q = (qt_s[...] * scale).T
    for i in range(group):
        out_ref[:, i * head_dim:(i + 1) * head_dim] = out[i * cap:(i + 1) * cap].astype(bf16)
        out_ref[:, width + i * head_dim:width + (i + 1) * head_dim] = (
            grad_q[i * cap:(i + 1) * cap].astype(bf16)
        )


def call(body, micros, ins, outs, scratch, limit, scalars=1):
    smem = pl.BlockSpec(memory_space=pltpu.SMEM)
    vmem = pl.BlockSpec(memory_space=pltpu.VMEM)
    return pl.pallas_call(
        body,
        out_shape=outs,
        in_specs=[smem] * scalars + [vmem] * (len(ins) - scalars),
        out_specs=[vmem] * len(outs),
        scratch_shapes=scratch,
        compiler_params=pltpu.CompilerParams(vmem_limit_bytes=limit * 1024 * 1024),
        cost_estimate=pl.CostEstimate(
            flops=int(micros * 1.15e9),
            bytes_accessed=sum(x.size * x.dtype.itemsize for x in ins + outs),
            transcendentals=0,
        ),
    )(*ins)


def near_stats(lengths, x, shards, group, scale):
    cap = x.shape[0]
    _, span, head_dim = shards[0].shape
    rows = group * cap
    return call(
        functools.partial(near_stats_kernel, group, len(shards), scale),
        2,
        [lengths, x, *shards],
        [jax.ShapeDtypeStruct((3, rows), f32)],
        [VMEM((rows, head_dim), bf16)] * 2,
        12,
    )[0]


def far_pass(lengths, x, stats, shards, group, scale):
    cap = x.shape[0]
    span, head_dim = shards[0].shape[2:]
    chunks = 2 * len(shards)
    rows, keys = group * cap, chunks * span
    outs = call(
        functools.partial(far_kernel, group, chunks, scale),
        6.5,
        [lengths, x, stats, *shards],
        [jax.ShapeDtypeStruct(shard.shape, bf16) for shard in shards]
        + [jax.ShapeDtypeStruct((2, rows), f32)]
        + [jax.ShapeDtypeStruct((head_dim, rows), f32)] * 2,
        [VMEM((rows, head_dim), bf16)] * 2
        + [VMEM((head_dim, keys), bf16)] * 2
        + [VMEM((keys, 256), f32)] * 2
        + [VMEM((keys, 256), bf16)] * 2
        + [VMEM((keys, head_dim), f32)] * 2,
        24,
    )
    return outs[:len(shards)], outs[len(shards):]


def near_pass(lengths, x, totals, shards, group, scale):
    cap, packed = x.shape
    _, span, head_dim = shards[0].shape
    rows, keys = group * cap, len(shards) * span + cap
    outs = call(
        functools.partial(near_kernel, group, len(shards), scale),
        5,
        [lengths, x, *totals, *shards],
        [jax.ShapeDtypeStruct((cap, packed), bf16)]
        + [jax.ShapeDtypeStruct(shard.shape, f32) for shard in shards],
        [VMEM((rows, head_dim), bf16)] * 2
        + [VMEM((head_dim, keys), bf16)] * 2
        + [VMEM((keys, 256), bf16)] * 2
        + [VMEM((head_dim, rows), f32)] * 2
        + [VMEM((keys, head_dim), f32)] * 2,
        24,
    )
    return outs[0], outs[1:]


def pair_kernel(first_ref, second_ref, out_ref):
    out_ref[0] = first_ref[...]
    out_ref[1] = second_ref[...]


def pair_up(held):
    shape = (len(held),) + held[0].shape
    return call(
        pair_kernel, 12, list(held), [jax.ShapeDtypeStruct(shape, bf16)], [], 8, scalars=0
    )[0]


def sum_kernel(count, *refs):
    for i in range(count):
        total = refs[i][...]
        for ref in refs[count:-count]:
            total = total + ref[i].astype(f32)
        refs[i - count][...] = total.astype(bf16)


def add_parts(held, parts):
    return call(
        functools.partial(sum_kernel, len(held)), 12, [*held, *parts],
        [jax.ShapeDtypeStruct(part.shape, bf16) for part in held], [], 8, scalars=0,
    )


def on_device(comp_q, comp_k, comp_v, comp_grad, prefix_k, prefix_v, comp_len):
    _, slots, heads, width = comp_q.shape
    head_dim = comp_k.shape[3]
    group = width // head_dim
    devices = lax.axis_size("seq")
    ring = devices // PROMPTS
    scale = 1.0 / math.sqrt(head_dim)

    holders = []
    for owner in range(devices):
        plane, lane = divmod(owner, PROMPTS)
        reach = (0, 3, 1, 2)[lane]
        holders.append((plane + reach if plane % 2 else plane - reach) % ring)

    def spread(steps):
        return [
            (owner, (holder + steps) % ring * PROMPTS + owner // ring)
            for owner, holder in enumerate(holders)
        ]

    def collect(x, steps):
        return lax.ppermute(x, "seq", [(b, a) for a, b in spread(steps)])

    def shift(x, steps):
        way = (PROMPTS * steps, -PROMPTS * steps)
        pairs = [(s, (s + way[s % 2]) % devices) for s in range(devices)]
        return lax.ppermute(x, "seq", pairs)

    half = ring // 2
    prefix = jnp.stack([prefix_k[:, 0], prefix_v[:, 0]])
    own, across = [lax.ppermute(prefix, "seq", spread(steps)) for steps in (0, half)]
    packed = pack(comp_q, comp_grad, comp_k, comp_v)
    own, across, _ = lax.optimization_barrier((own, across, packed))
    x = lax.all_to_all(packed, "head", split_axis=0, concat_axis=0, tiled=True)

    held, steps = [own, across], (1, -1, 2)
    both = pair_up(held)
    far = [shift(both, step) for step in steps]
    stats = near_stats(comp_len, x, held, group, scale)
    grads, totals = far_pass(comp_len, x, stats, far, group, scale)
    moved = [shift(grad, -step) for grad, step in zip(grads, steps)]
    out, held_grads = near_pass(comp_len, x, totals, held, group, scale)
    own, across = add_parts(held_grads, moved)
    back = lax.all_to_all(out, "head", split_axis=0, concat_axis=0, tiled=True)
    attn_out, grad_q, grad_k, grad_v = unpack(back, heads, width, head_dim)
    own, across = collect(own, 0), collect(across, half)
    own, across, (attn_out, grad_q, grad_k, grad_v) = lax.optimization_barrier(
        (own, across, (attn_out, grad_q, grad_k, grad_v))
    )
    placed = [own[i].astype(f32) + across[i].astype(f32) for i in range(2)]
    return (attn_out, grad_q, grad_k, grad_v, placed[0][:, None], placed[1][:, None])


def solution(mesh):
    tokens = P("seq", "head", None, None)
    prefix = P("seq", "head", None)
    return jax.shard_map(
        on_device,
        mesh=mesh,
        in_specs=(tokens, tokens, tokens, tokens, prefix, prefix, P()),
        out_specs=(tokens, tokens, tokens, tokens, prefix, prefix),
        check_vma=False,
    )
```
